128 devices in a mesh: replica: 8 (over x_hi, z), fsdp: 16 (over y, x_lo, core).
Axes of the slice: x: 4 (x_hi: 2, x_lo: 2; x = x_hi * 2 + x_lo), y: 4, z: 4, core: 2. Of those that a mesh axis runs over, the one named last changes fastest.
Arguments:
- inner_weight: float32 [8, 4608, 2048], P('replica', 'fsdp'), may hold values from -6 to 6
- first_moment: float32 [8, 4608, 2048], P('replica', 'fsdp'), may hold values from -4 to 4
- second_moment: float32 [8, 4608, 2048], P('replica', 'fsdp'), may hold values from 0.01 to 2
- outer_weight: float32 [4608, 2048], P('fsdp', 'replica'), may hold values from -6 to 6
- outer_momentum: float32 [4608, 2048], P('fsdp', 'replica'), may hold values from -4 to 4
- activations: bfloat16 [8, 8192, 4608], P('replica', 'fsdp'), may hold values from -6 to 6
- out_grads: bfloat16 [8, 8192, 2048], P('replica', 'fsdp'), may hold values from -0.0625 to 0.0625
Outputs:
- inner_next: float32 [8, 4608, 2048], P('replica', 'fsdp')
- first_next: float32 [8, 4608, 2048], P('replica', 'fsdp')
- second_next: float32 [8, 4608, 2048], P('replica', 'fsdp')
- outer_next: float32 [4608, 2048], P('fsdp', 'replica')
- momentum_next: float32 [4608, 2048], P('fsdp', 'replica')
The draws below stay inside these ranges and needn't reach their ends.
All inputs are finite; a program needn't handle non-finite values.
Results may differ from the reference program's by a relative error of at most 0.0003.
Values may be sent and summed in bfloat16 or wider, within the bound.
No kernel may reach another device: no remote copies, remote signals or barrier semaphores. Data moves between devices by JAX's collectives and lax.ppermute only.
A program may use at most 128 MiB of HBM per device.

```python
import math
import jax
import jax.numpy as jnp
from jax import lax

D = 4608
F = 2048
REPLICAS = 8
TOKENS = 8192


def strengthened(entries, rng, source, target, shards_of, factor):
    def block_of(dim):
        return (jnp.arange(entries.shape[dim]) // (entries.shape[dim] // shards_of)).reshape((-1,) + (1,) * (entries.ndim - 1 - dim))

    near = jax.random.permutation(rng, shards_of)[block_of(target)]
    second = (block_of(target) + shards_of // 2) % shards_of
    return jnp.where((block_of(source) == near) | (block_of(source) == second), factor * entries, entries)


def steps_of(own_key, shape, cuts, low, high):
    gain, own = 1.0, jax.random.fold_in(own_key, 6)
    for dim, shards_of in cuts:
        draws = jnp.exp(jax.random.uniform(jax.random.fold_in(own, dim), (shards_of,), jnp.float32, low / len(cuts), high / len(cuts)))
        gain = gain * jnp.repeat(draws, shape[dim] // shards_of).reshape([-1 if axis == dim else 1 for axis in range(len(shape))])
    return gain


def normal_values(stream_key, shape, scale, most, split=(), kind=jnp.bfloat16):
    drawn = jax.random.normal(stream_key, shape, jnp.float32) * scale
    if len(split) > 0:
        drawn = steps_of(stream_key, shape, split, -0.22, 0.18) * drawn
    return jnp.clip(drawn, min=-most, max=most).astype(kind)


def bell_draw_with(rng, dims, width, bound, pieces, heavy, held_as=jnp.bfloat16):
    drawn = width * jax.random.normal(rng, dims, jnp.float32)
    if pieces:
        drawn = drawn * steps_of(rng, dims, pieces, -0.22, 0.18)
    return jnp.clip(strengthened(drawn, jax.random.fold_in(rng, 3), *heavy), -bound, bound).astype(held_as)


def setup_inputs(seed: int = 0) -> dict:
    key_of = jax.random.split(jax.random.key(seed), 8)
    inner_weight = bell_draw_with(key_of[0], (REPLICAS, D, F), 1.0, 6.0, ((0, 8), (1, 16)), (0, 2, 8, 2.0), jnp.float32)
    first_moment = normal_values(key_of[1], (REPLICAS, D, F), 0.5, 4.0, ((0, 8), (1, 16)), jnp.float32)
    second_moment = jnp.clip(jnp.exp(math.log(2.0) - 5.2983174 * jax.random.uniform(key_of[2], (REPLICAS, D, F), jnp.float32) ** steps_of(key_of[2], (REPLICAS, D, F), ((0, 8), (1, 16)), -0.2, 0.2)), 0.01, 2.0)
    outer_weight = normal_values(key_of[3], (D, F), 1.0, 6.0, ((0, 16), (1, 8)), jnp.float32)
    outer_momentum = normal_values(key_of[4], (D, F), 0.5, 4.0, ((0, 16), (1, 8)), jnp.float32)
    activations = bell_draw_with(key_of[5], (REPLICAS, TOKENS, D), 1.0, 6.0, ((0, 8), (1, 16)), (1, 2, 16, 2.0))
    out_grads = normal_values(key_of[6], (REPLICAS, TOKENS, F), TOKENS ** -0.5, 0.0625, ((0, 8), (1, 16)))
    return dict(inner_weight=inner_weight, first_moment=first_moment, second_moment=second_moment, outer_weight=outer_weight, outer_momentum=outer_momentum, activations=activations, out_grads=out_grads)


outer_rate = 0.7
outer_decay = 0.9
mix_share = 0.5
beta_one = 0.9
beta_two = 0.95
inner_rate = 0.05
weight_decay = 0.1
epsilon = 1e-08
step_count = 200.0

def replica_grad(pair):
    inputs, cotangents = pair
    return lax.dot_general(inputs, cotangents, (((0,), (0,)), ((), ())), preferred_element_type=jnp.float32)

def reference(inner_weight, first_moment, second_moment, outer_weight, outer_momentum, activations, out_grads):
    summed = lax.optimization_barrier(jnp.sum(inner_weight, axis=0))
    average = outer_weight - summed / REPLICAS
    momentum_next = outer_decay * outer_momentum + average
    outer_next = outer_weight - outer_rate * (average + outer_decay * momentum_next)
    blended = mix_share * outer_next[None] + (1.0 - mix_share) * inner_weight
    grad = lax.map(replica_grad, (activations, out_grads))
    first_next = beta_one * first_moment + (1.0 - beta_one) * grad
    second_next = beta_two * second_moment + (1.0 - beta_two) * grad * grad
    corr_one = 1.0 - beta_one ** step_count
    corr_two = 1.0 - beta_two ** step_count
    update = first_next / corr_one / (jnp.sqrt(second_next / corr_two) + epsilon)
    inner_next = blended - inner_rate * (update + weight_decay * blended)
    return (inner_next, first_next, second_next, outer_next, momentum_next)
```

```python
import functools

import jax
import jax.numpy as jnp
from jax import lax
from jax.experimental import pallas as pl
from jax.experimental.pallas import tpu as pltpu
from jax.sharding import PartitionSpec as P

outer_rate = 0.7
outer_decay = 0.9
mix_share = 0.5
beta_one = 0.9
beta_two = 0.95
inner_rate = 0.05
weight_decay = 0.1
epsilon = 1e-08
step_count = 200.0
corr_one = 1.0 - beta_one**step_count
corr_two = 1.0 - beta_two**step_count

NY, NX, NC, NZ, NH = 4, 2, 2, 4, 2
WA, B1, B2 = 640, 256, 512
CA, CB = 2 * WA, B1 + B2
ORDER = (2, 1, 3, 0)
VMEM = 40 * 2**20


def along_fsdp(move):
    where = [(y, x, c) for y in range(NY) for x in range(NX) for c in range(NC)]
    number = lambda y, x, c: ((y % NY) * NX + x) * NC + c
    return [(number(*place), number(*move(*place))) for place in where]


def along_replica(move):
    where = [(h, z) for h in range(NH) for z in range(NZ)]
    number = lambda h, z: h * NZ + z % NZ
    return [(number(*place), number(*move(*place))) for place in where]


UP = along_fsdp(lambda y, x, c: (y + 1, x, c))
DOWN = along_fsdp(lambda y, x, c: (y - 1, x, c))
ACROSS = along_fsdp(lambda y, x, c: (y, 1 - x, c))
TWIN = along_fsdp(lambda y, x, c: (y, x, 1 - c))
FAR = along_replica(lambda h, z: (1 - h, z))
AHEAD = [along_replica(lambda h, z, k=k: (h, z + k)) for k in range(NZ)]


def on_fsdp(value, pairs):
    return lax.ppermute(value, "fsdp", pairs)


def on_replica(value, pairs):
    return lax.ppermute(value, "replica", pairs)


def coded(value):
    return (value * jnp.abs(value) * (value * value)).astype(jnp.bfloat16)


def decoded(code):
    code = code.astype(jnp.float32)
    root = lax.rsqrt(lax.rsqrt(jnp.abs(code)))
    return jnp.where(code < 0.0, -root, root)


def coded_outer(value):
    value = value * 4096.0
    square = value * value
    fourth = square * square
    return (value * jnp.abs(value) * square * fourth).astype(jnp.bfloat16)


def decoded_outer(code):
    code = code.astype(jnp.float32)
    root = jnp.sqrt(lax.rsqrt(lax.rsqrt(jnp.abs(code)))) * (1.0 / 4096.0)
    return jnp.where(code < 0.0, -root, root)


def params(vmem=VMEM):
    return pltpu.CompilerParams(vmem_limit_bytes=vmem)


def cost(flops, moved):
    return pl.CostEstimate(flops=int(flops), bytes_accessed=int(moved), transcendentals=0)


def prepare(place, activations, distances):
    tokens, width = activations.shape
    quarter = width // NY
    rows = quarter // (NX * NC)
    first, count = distances

    def distance(i):
        step = first + i
        return jnp.where(step == 0, 2, jnp.where(step == 1, 1, jnp.where(step == 2, 3, 0)))

    def kernel(place_ref, a_ref, own_ref, send_ref, turned):
        turned[...] = a_ref[...].T
        x, core = place_ref[1], place_ref[2]
        for dx in range(NX):
            column = (x + dx) % NX
            own = pl.multiple_of((column * NC + core) * rows, 16)
            other = pl.multiple_of((column * NC + 1 - core) * rows, 16)
            own_ref[dx] = turned[pl.ds(own, rows), :]
            send_ref[dx] = turned[pl.ds(other, rows), :]

    shape = jax.ShapeDtypeStruct((NX * count, rows, tokens), jnp.bfloat16)
    spec = pl.BlockSpec((NX, rows, tokens), lambda i, s: (i, 0, 0))
    return pl.pallas_call(
        kernel,
        out_shape=(shape, shape),
        grid_spec=pltpu.PrefetchScalarGridSpec(
            num_scalar_prefetch=1,
            grid=(count,),
            in_specs=[pl.BlockSpec((tokens, quarter), lambda i, s: (0, (s[0] + distance(i)) % NY))],
            out_specs=(spec, spec),
            scratch_shapes=[pltpu.VMEM((quarter, tokens), jnp.bfloat16)],
        ),
        compiler_params=params(),
        cost_estimate=cost(0, 2 * tokens * quarter * count * 2),
    )(place, activations)


def multiplied(left_own, left_twin, right_own, right_twin):
    return jnp.dot(left_own, right_own, preferred_element_type=jnp.float32) + jnp.dot(
        left_twin, right_twin, preferred_element_type=jnp.float32
    )


def product(lefts, rights, blocks, columns, received=()):
    start, step, count = blocks
    width, place = columns
    rows, depth = lefts[0].shape[1:]

    def kernel(lo, lt, ro, rt, *rest):
        out = rest[-1]
        total = multiplied(lo[0], lt[0], ro[...], rt[...])
        for code in rest[:-1]:
            total = total + decoded(code[0])
        out[0] = coded(total)

    left = pl.BlockSpec((1, rows, depth), lambda i: (start + step * i, 0, 0))
    right = pl.BlockSpec((depth, width), lambda i: (0, place))
    block = pl.BlockSpec((1, rows, width), lambda i: (i, 0, 0))
    return pl.pallas_call(
        kernel,
        out_shape=jax.ShapeDtypeStruct((count, rows, width), jnp.bfloat16),
        grid=(count,),
        in_specs=[left, left, right, right] + [block] * len(received),
        out_specs=block,
        compiler_params=params(),
        cost_estimate=cost(
            4 * count * rows * width * depth,
            4 * depth * (count * rows + width) + 2 * count * rows * width * (1 + len(received)),
        ),
    )(*lefts, *rights, *received)


def narrow(lefts, rights, blocks):
    start, step, count = blocks
    rows, depth = lefts[0].shape[1:]

    def kernel(lo, lt, ro1, rt1, ro2, rt2, out):
        out[0, :, :B1] = coded(multiplied(lo[0], lt[0], ro1[...], rt1[...]))
        out[0, :, B1:] = coded(multiplied(lo[0], lt[0], ro2[...], rt2[...]))

    left = pl.BlockSpec((1, rows, depth), lambda i: (start + step * i, 0, 0))
    near = pl.BlockSpec((depth, B1), lambda i: (0, CA // B1))
    far = pl.BlockSpec((depth, B2), lambda i: (0, (CA + B1) // B2))
    return pl.pallas_call(
        kernel,
        out_shape=jax.ShapeDtypeStruct((count, rows, CB), jnp.bfloat16),
        grid=(count,),
        in_specs=[left, left, near, near, far, far],
        out_specs=pl.BlockSpec((1, rows, CB), lambda i: (i, 0, 0)),
        compiler_params=params(),
        cost_estimate=cost(
            4 * count * rows * CB * depth, 4 * depth * (count * rows + CB) + 2 * count * rows * CB
        ),
    )(*lefts, *rights, *rights)


def middle(lefts, rights, block, columns, inner_half, across, received=()):
    rows, depth = lefts[0].shape[1:]
    width, place = columns
    row_block, = inner_half

    def kernel(lo, lt, ro, rt, code, *rest):
        out = rest[-1]
        total = multiplied(lo[0], lt[0], ro[...], rt[...])
        sent = code[0, :, :B1] if width == B1 else code[0, :, B1:]
        total = total + decoded(sent)
        for more in rest[:-1]:
            total = total + decoded(more[...])
        out[...] = coded(total)

    left = pl.BlockSpec((1, rows, depth), lambda i: (block, 0, 0))
    right = pl.BlockSpec((depth, width), lambda i: (0, place))
    whole = pl.BlockSpec((rows, width), lambda i: (0, 0))
    return pl.pallas_call(
        kernel,
        out_shape=jax.ShapeDtypeStruct((rows, width), jnp.bfloat16),
        grid=(1,),
        in_specs=[left, left, right, right, pl.BlockSpec((1, rows, CB), lambda i: (row_block, 0, 0))]
        + [whole] * len(received),
        out_specs=whole,
        compiler_params=params(),
        cost_estimate=cost(4 * rows * width * depth, 4 * depth * (rows + width) + 8 * rows * width),
    )(*lefts, *rights, across, *received)


def turn(lefts, rights, received):
    rows, depth = lefts[0].shape[1:]
    block = lefts[0].shape[0] - 1

    def kernel(lo, lt, ro, rt, *rest):
        out = rest[-1]
        total = multiplied(lo[0], lt[0], ro[...], rt[...])
        first, second = rest[0], rest[1]
        half = pl.program_id(0)

        @pl.when(half == 0)
        def _():
            out[...] = coded(total + decoded(rest[0][0]) + decoded(rest[1][0]))

        @pl.when(half == 1)
        def _():
            out[...] = coded(total + decoded(rest[2][0]) + decoded(rest[3][0]))

    left = pl.BlockSpec((1, rows, depth), lambda i: (block, 0, 0))
    right = pl.BlockSpec((depth, WA), lambda i: (0, i))
    code = pl.BlockSpec((1, rows, WA), lambda i: (1, 0, 0))
    return pl.pallas_call(
        kernel,
        out_shape=jax.ShapeDtypeStruct((rows, CA), jnp.bfloat16),
        grid=(2,),
        in_specs=[left, left, right, right] + [code] * 4,
        out_specs=pl.BlockSpec((rows, WA), lambda i: (0, i)),
        compiler_params=params(),
        cost_estimate=cost(4 * rows * CA * depth, 4 * depth * (rows + CA) + 10 * rows * CA),
    )(*lefts, *rights, *received)


def adam(total, blended, first, second, inner_out, first_out, second_out):
    first_next = beta_one * first + (1.0 - beta_one) * total
    second_next = beta_two * second + (1.0 - beta_two) * total * total
    update = first_next / corr_one / (jnp.sqrt(second_next / corr_two) + epsilon)
    inner_out[...] = blended - inner_rate * (update + weight_decay * blended)
    first_out[...] = first_next
    second_out[...] = second_next


def finish(lefts, rights, columns, codes, states, outs):
    rows, depth = lefts[0].shape[1:]
    block = lefts[0].shape[0] - 2
    width, place = columns
    cuts = 3
    part = rows // cuts
    n = len(codes)

    def kernel(lo, lt, ro, rt, *rest):
        total = multiplied(lo[0], lt[0], ro[...], rt[...])
        for code in rest[:n]:
            value = code[0] if len(code.shape) == 3 else code[...]
            total = total + decoded(value)
        blended, first, second = rest[n : n + 3]
        adam(total, blended[...], first[...], second[...], *rest[-3:])

    left = pl.BlockSpec((1, part, depth), lambda i: (block, i, 0))
    right = pl.BlockSpec((depth, width), lambda i: (0, place))
    state = pl.BlockSpec((part, width), lambda i: (i, place))
    specs = []
    for array, at in codes:
        if array.ndim == 3:
            specs.append(pl.BlockSpec((1, part, width), lambda i, at=at: (at[0], i, at[1])))
        else:
            specs.append(pl.BlockSpec((part, width), lambda i, at=at: (i, at[1])))
    arrays = [array for array, _ in codes]
    shape = jax.ShapeDtypeStruct(states[0].shape, jnp.float32)
    operands = [*lefts, *rights, *arrays, *states]
    aliases = {}
    if outs is not None:
        aliases = {len(operands) + i: i for i in range(3)}
        operands += list(outs)
    return pl.pallas_call(
        (lambda *refs: kernel(*refs[: 7 + n], *refs[-3:])),
        out_shape=(shape,) * 3,
        grid=(cuts,),
        in_specs=[left, left, right, right]
        + specs
        + [state] * 3
        + ([pl.BlockSpec(memory_space=pl.ANY)] * 3 if outs is not None else []),
        out_specs=(state,) * 3,
        input_output_aliases=aliases,
        compiler_params=params(),
        cost_estimate=cost(4 * rows * width * depth, 4 * depth * (rows + width) + 32 * rows * width),
    )(*operands)


def scatter_blocks(place, inner):
    rows, width = inner.shape
    block = width // (NZ * NH)

    def kernel(place_ref, *refs):
        for source, target in zip(refs[: NZ - 1], refs[NZ - 1 :]):
            target[0] = source[...]

    def source(k):
        return pl.BlockSpec(
            (rows, block), lambda i, s: (0, ((s[4] + i) % NH) * NZ + (s[3] + k) % NZ)
        )

    shape = jax.ShapeDtypeStruct((NH, rows, block), jnp.float32)
    target = pl.BlockSpec((1, rows, block), lambda i, s: (i, 0, 0))
    return pl.pallas_call(
        kernel,
        out_shape=(shape,) * (NZ - 1),
        grid_spec=pltpu.PrefetchScalarGridSpec(
            num_scalar_prefetch=1,
            grid=(NH,),
            in_specs=[source(k) for k in range(1, NZ)],
            out_specs=(target,) * (NZ - 1),
        ),
        compiler_params=params(),
        cost_estimate=cost(0, 8 * (NZ - 1) * NH * rows * block),
    )(place, inner, inner, inner)


def sum_far(place, inner, received):
    rows, width = inner.shape
    block = width // (NZ * NH)

    def kernel(place_ref, own, a, b, c, out):
        out[...] = own[...] + a[0] + b[0] + c[0]

    code = pl.BlockSpec((1, rows, block), lambda i, s: (1, 0, 0))
    return pl.pallas_call(
        kernel,
        out_shape=jax.ShapeDtypeStruct((rows, block), jnp.float32),
        grid_spec=pltpu.PrefetchScalarGridSpec(
            num_scalar_prefetch=1,
            grid=(1,),
            in_specs=[pl.BlockSpec((rows, block), lambda i, s: (0, ((s[4] + 1) % NH) * NZ + s[3]))]
            + [code] * 3,
            out_specs=pl.BlockSpec((rows, block), lambda i, s: (0, 0)),
        ),
        compiler_params=params(),
        cost_estimate=cost(0, 20 * rows * block),
    )(place, inner, *received)


def outer_step(place, inner, received, far, outer_weight, outer_momentum):
    rows, width = inner.shape
    block = width // (NZ * NH)

    def kernel(place_ref, own, a, b, c, far_ref, weight, momentum, next_ref, momentum_ref, code_ref):
        summed = own[...] + a[0] + b[0] + c[0] + far_ref[...]
        average = weight[...] - summed / (NZ * NH)
        momentum_next = outer_decay * momentum[...] + average
        outer_next = weight[...] - outer_rate * (average + outer_decay * momentum_next)
        next_ref[...] = outer_next
        momentum_ref[...] = momentum_next
        code_ref[...] = coded_outer(outer_next)

    code = pl.BlockSpec((1, rows, block), lambda i, s: (0, 0, 0))
    whole = pl.BlockSpec((rows, block), lambda i, s: (0, 0))
    shape = jax.ShapeDtypeStruct((rows, block), jnp.float32)
    return pl.pallas_call(
        kernel,
        out_shape=(shape, shape, jax.ShapeDtypeStruct((rows, block), jnp.bfloat16)),
        grid_spec=pltpu.PrefetchScalarGridSpec(
            num_scalar_prefetch=1,
            grid=(1,),
            in_specs=[pl.BlockSpec((rows, block), lambda i, s: (0, s[4] * NZ + s[3]))]
            + [code] * 3
            + [whole] * 3,
            out_specs=(whole,) * 3,
        ),
        compiler_params=params(),
        cost_estimate=cost(0, 38 * rows * block),
    )(place, inner, *received, far, outer_weight, outer_momentum)


def blend(place, inner, gathered):
    rows, width = inner.shape
    block = width // (NZ * NH)

    def kernel(place_ref, inner_ref, *refs):
        out = refs[-1]
        j = pl.program_id(0)
        back = (place_ref[3] - j % NZ + NZ) % NZ
        side = (j // NZ + place_ref[4]) % NH
        for k in range(NZ):

            @pl.when(back == k)
            def _():
                outer = decoded_outer(refs[k][side])
                out[...] = mix_share * outer + (1.0 - mix_share) * inner_ref[...]

    whole = pl.BlockSpec((NH, rows, block), lambda j, s: (0, 0, 0))
    state = pl.BlockSpec((rows, block), lambda j, s: (0, j))
    return pl.pallas_call(
        kernel,
        out_shape=jax.ShapeDtypeStruct((rows, width), jnp.float32),
        grid_spec=pltpu.PrefetchScalarGridSpec(
            num_scalar_prefetch=1,
            grid=(NZ * NH,),
            in_specs=[state] + [whole] * NZ,
            out_specs=state,
        ),
        compiler_params=params(),
        cost_estimate=cost(0, 10 * rows * width),
    )(place, inner, *gathered)


def local(
    inner_weight, first_moment, second_moment, outer_weight, outer_momentum, activations, out_grads
):
    inner, first, second = inner_weight[0], first_moment[0], second_moment[0]
    inputs, cotangents = activations[0], out_grads[0]
    replica, member = lax.axis_index("replica"), lax.axis_index("fsdp")
    core, column, row = member % NC, member // NC % NX, member // (NC * NX)
    depth, side = replica % NZ, replica // NZ
    place = jnp.stack([row, column, core, depth, side]).astype(jnp.int32)

    rights = (cotangents, on_fsdp(cotangents, TWIN))
    far_own, far_send = prepare(place, inputs, (0, 1))
    far_left = (far_own, on_fsdp(far_send, TWIN))
    near_own, near_send = prepare(place, inputs, (1, 3))
    near_left = (near_own, on_fsdp(near_send, TWIN))

    blocks = scatter_blocks(place, inner)
    arrived = [on_replica(blocks[k - 1], AHEAD[k]) for k in range(1, NZ)]

    up_far = on_fsdp(product(far_left, rights, (0, 1, 2), (WA, 0)), UP)
    down_far = on_fsdp(product(far_left, rights, (0, 1, 2), (WA, 1)), DOWN)
    across_far = on_fsdp(narrow(far_left, rights, (1, 1, 1)), ACROSS)
    up_own = on_fsdp(product(near_left, rights, (0, 1, 2), (WA, 1)), UP)
    down_own = on_fsdp(product(near_left, rights, (2, 1, 2), (WA, 0)), DOWN)
    across_near = on_fsdp(narrow(near_left, rights, (1, 2, 2)), ACROSS)
    across_here = on_fsdp(narrow(near_left, rights, (5, 1, 1)), ACROSS)

    up_both = on_fsdp(product(near_left, rights, (0, 1, 2), (WA, 0), (up_far,)), UP)
    down_both = on_fsdp(product(near_left, rights, (2, 1, 2), (WA, 1), (down_far,)), DOWN)

    far_sum = on_replica(sum_far(place, inner, arrived), FAR)
    outer_next, momentum_next, code = outer_step(
        place, inner, arrived, far_sum, outer_weight, outer_momentum
    )
    pair = jnp.stack([code, on_replica(code, FAR)])
    gathered = [pair] + [on_replica(pair, AHEAD[k]) for k in range(1, NZ)]

    half_one, half_two = (B1, CA // B1), (B2, (CA + B1) // B2)
    up_first = on_fsdp(middle(far_left, rights, 0, half_one, (0,), across_far), UP)
    down_first = on_fsdp(middle(far_left, rights, 0, half_two, (0,), across_far), DOWN)
    up_second = on_fsdp(middle(near_left, rights, 0, half_two, (0,), across_near), UP)
    down_second = on_fsdp(middle(near_left, rights, 2, half_one, (1,), across_near), DOWN)

    turned = turn(near_left, rights, (up_both, down_own, up_own, down_both))
    across_turned = on_fsdp(turned, ACROSS)

    up_third = on_fsdp(
        middle(near_left, rights, 0, half_one, (0,), across_near, (up_first,)), UP
    )
    down_third = on_fsdp(
        middle(near_left, rights, 2, half_two, (1,), across_near, (down_first,)), DOWN
    )

    blended = blend(place, inner, gathered)
    states = (blended, first, second)
    here_one, here_two = across_here[0, :, :B1], across_here[0, :, B1:]
    outs = finish(
        near_left, rights, half_one,
        [(here_one, (0, 0)), (up_third, (0, 0)), (down_second, (0, 0))], states, None,
    )
    outs = finish(
        near_left, rights, half_two,
        [(here_two, (0, 0)), (up_second, (0, 0)), (down_third, (0, 0))], states, outs,
    )
    outs = finish(
        near_left, rights, (WA, 0),
        [(up_both, (0, 0)), (down_own, (0, 0)), (across_turned, (0, 0))], states, outs,
    )
    outs = finish(
        near_left, rights, (WA, 1),
        [(up_own, (0, 0)), (down_both, (0, 0)), (across_turned, (0, 1))], states, outs,
    )
    inner_next, first_next, second_next = outs
    return (inner_next[None], first_next[None], second_next[None], outer_next, momentum_next)


def solution(mesh):
    in_specs = (
        P("replica", "fsdp", None),
        P("replica", "fsdp", None),
        P("replica", "fsdp", None),
        P("fsdp", "replica"),
        P("fsdp", "replica"),
        P("replica", "fsdp", None),
        P("replica", "fsdp", None),
    )
    out_specs = (
        P("replica", "fsdp", None),
        P("replica", "fsdp", None),
        P("replica", "fsdp", None),
        P("fsdp", "replica"),
        P("fsdp", "replica"),
    )
    return jax.shard_map(local, mesh=mesh, in_specs=in_specs, out_specs=out_specs, check_vma=False)
```

```python
import jax
import jax.numpy as jnp
from jax import lax
from jax.experimental import pallas as pl
from jax.experimental.pallas import tpu as pltpu
from jax.sharding import PartitionSpec as P

outer_rate = 0.7
outer_decay = 0.9
mix_share = 0.5
beta_one = 0.9
beta_two = 0.95
inner_rate = 0.05
weight_decay = 0.1
epsilon = 1e-08
step_count = 200.0
corr_one = 1.0 - beta_one**step_count
corr_two = 1.0 - beta_two**step_count

NY, NX, NC, NZ, NH = 4, 2, 2, 4, 2
BLOCK = 256
A1, A2, B1, B2 = (0, 3), (3, 3), (6, 1), (7, 1)
A, B, ALL = (0, 6), (6, 2), (0, 8)
VMEM = 16 * 2**20


def along_fsdp(move):
    where = [(y, x, c) for y in range(NY) for x in range(NX) for c in range(NC)]
    number = lambda y, x, c: ((y % NY) * NX + x) * NC + c
    return [(number(*place), number(*move(*place))) for place in where]


def along_replica(move):
    where = [(h, z) for h in range(NH) for z in range(NZ)]
    number = lambda h, z: h * NZ + z % NZ
    return [(number(*place), number(*move(*place))) for place in where]


UP = along_fsdp(lambda y, x, c: (y + 1, x, c))
DOWN = along_fsdp(lambda y, x, c: (y - 1, x, c))
ACROSS = along_fsdp(lambda y, x, c: (y, 1 - x, c))
TWIN = along_fsdp(lambda y, x, c: (y, x, 1 - c))
FAR = along_replica(lambda h, z: (1 - h, z))
AHEAD = [along_replica(lambda h, z, k=k: (h, z + k)) for k in range(NZ)]


def on_fsdp(value, pairs):
    return lax.ppermute(value, "fsdp", pairs)


def on_replica(value, pairs):
    return lax.ppermute(value, "replica", pairs)


def coded(value):
    return (value * jnp.abs(value) * (value * value)).astype(jnp.bfloat16)


def decoded(code):
    code = code.astype(jnp.float32)
    root = lax.rsqrt(lax.rsqrt(jnp.abs(code)))
    return jnp.where(code < 0.0, -root, root)


def coded_outer(value):
    value = value * 4096.0
    square = value * value
    fourth = square * square
    return (value * jnp.abs(value) * square * fourth).astype(jnp.bfloat16)


def decoded_outer(code):
    code = code.astype(jnp.float32)
    root = jnp.sqrt(lax.rsqrt(lax.rsqrt(jnp.abs(code)))) * (1.0 / 4096.0)
    return jnp.where(code < 0.0, -root, root)


def run(kernel, grid, ins, outs, after=(), prefetch=(), scratch=(), aliases=None):
    read, late = len(prefetch) + len(ins), len(after)

    def body(*refs):
        kernel(*refs[:read], *refs[read + late :])

    arrays = [array for array, _ in ins]
    shapes = tuple(shape for shape, _ in outs)
    result = pl.pallas_call(
        body,
        out_shape=shapes,
        grid_spec=pltpu.PrefetchScalarGridSpec(
            num_scalar_prefetch=len(prefetch),
            grid=grid,
            in_specs=[spec for _, spec in ins] + [pl.BlockSpec(memory_space=pl.ANY)] * late,
            out_specs=tuple(spec for _, spec in outs),
            scratch_shapes=list(scratch),
        ),
        input_output_aliases=aliases or {},
        compiler_params=pltpu.CompilerParams(vmem_limit_bytes=VMEM),
        cost_estimate=pl.CostEstimate(flops=1, bytes_accessed=1, transcendentals=0),
    )(*prefetch, *arrays, *after)
    return result[0] if len(outs) == 1 else result


def prepare(place, activations, first, count, after=()):
    tokens, width = activations.shape
    quarter = width // NY
    rows = quarter // (NX * NC)

    def distance(i):
        step = first + i
        return jnp.where(step == 0, 2, jnp.where(step == 1, 1, jnp.where(step == 2, 3, 0)))

    def kernel(place_ref, a_ref, own_ref, send_ref, turned):
        turned[...] = a_ref[...].T
        x, core = place_ref[1], place_ref[2]
        for dx in range(NX):
            column = (x + dx) % NX
            own = pl.multiple_of((column * NC + core) * rows, 16)
            other = pl.multiple_of((column * NC + 1 - core) * rows, 16)
            own_ref[dx, 0] = turned[pl.ds(own, rows), :]
            send_ref[dx, 0] = turned[pl.ds(other, rows), :]

    out = (
        jax.ShapeDtypeStruct((NX, count, rows, tokens), jnp.bfloat16),
        pl.BlockSpec((NX, 1, rows, tokens), lambda i, s: (0, i, 0, 0)),
    )
    source = pl.BlockSpec((tokens, quarter), lambda i, s: (0, (s[0] + distance(i)) % NY))
    own, send = run(
        kernel, (count,), [(activations, source)], [out, out], after, (place,),
        [pltpu.VMEM((quarter, tokens), jnp.bfloat16)],
    )
    return own.reshape(NX * count, rows, tokens), send.reshape(NX * count, rows, tokens)


def run_whole(kernel, arrays, shape, after=()):
    count = len(arrays)
    vmem = pl.BlockSpec(memory_space=pltpu.VMEM)

    def body(*refs):
        kernel(*refs[:count], refs[-1])

    return pl.pallas_call(
        body,
        out_shape=shape,
        in_specs=[vmem] * count + [pl.BlockSpec(memory_space=pl.ANY)] * len(after),
        out_specs=vmem,
        compiler_params=pltpu.CompilerParams(vmem_limit_bytes=VMEM),
    )(*arrays, *after)


def block_columns(j):
    start = j * BLOCK
    return pl.ds(start if isinstance(start, int) else pl.multiple_of(start, BLOCK), BLOCK)


def dots(lefts, rights, blocks, j):
    start, count = blocks
    total = None
    for left, right in zip(lefts, rights):
        rows, depth = left.shape[1:]
        part = left[start : start + count].reshape(count * rows, depth)
        part = jnp.dot(part, right[:, block_columns(j)], preferred_element_type=jnp.float32)
        total = part if total is None else total + part
    return total.reshape(count, rows, BLOCK)


def regions(number, received):
    cuts = {0, number}
    for _, _, span, _ in received:
        cuts |= {span[0], span[0] + span[1]}
    cuts = sorted(cuts)
    found = []
    for low, high in zip(cuts, cuts[1:]):
        which = [i for i, (_, _, span, _) in enumerate(received) if span[0] <= low < span[0] + span[1]]
        found.append((low, high, which))
    return found


def product(lefts, rights, blocks, columns, received=(), after=(), kind=jnp.bfloat16):
    first, number = columns
    count, rows = blocks[1], lefts[0].shape[1]

    def kernel(lo, lt, ro, rt, *rest):
        out = rest[-1]

        def step(j, which):
            total = dots((lo, lt), (ro, rt), blocks, first + j)
            for i in which:
                _, block, span, offset = received[i]
                total = total + decoded(rest[i][block : block + count, :, block_columns(offset + j - span[0])])
            out[:, :, block_columns(j)] = coded(total) if kind == jnp.bfloat16 else total

        for low, high, which in regions(number, received):
            pl.loop(low, high)(lambda j, which=which: step(j, which))

    shape = jax.ShapeDtypeStruct((count, rows, number * BLOCK), kind)
    return run_whole(kernel, [*lefts, *rights, *(array for array, *_ in received)], shape, after)


def product_pair(lefts, rights, block, columns, lefts_last, block_last, column_last, codes, after=()):
    first, number = columns
    rows = lefts[0].shape[1]

    def kernel(lo, lt, lo2, lt2, ro, rt, code, out):
        @pl.loop(0, number)
        def _(j):
            out[:, :, block_columns(j)] = coded(dots((lo, lt), (ro, rt), (block, 1), first + j))

        total = dots((lo2, lt2), (ro, rt), (block_last, 1), column_last)
        total = total + decoded(code[:, :, block_columns(column_last - B[0])])
        out[:, :, block_columns(number)] = coded(total)

    shape = jax.ShapeDtypeStruct((1, rows, (number + 1) * BLOCK), jnp.bfloat16)
    return run_whole(kernel, [*lefts, *lefts_last, *rights, codes], shape, after)


def finish(base, down, across, states, after=()):
    rows, width = states[0].shape
    wide = 2 * BLOCK

    def kernel(base_ref, down_ref, across_ref, blended_ref, first_ref, second_ref, inner_out, first_out, second_out):
        def store(total):
            first_next = beta_one * first_ref[...] + (1.0 - beta_one) * total
            second_next = beta_two * second_ref[...] + (1.0 - beta_two) * total * total
            scaled = second_next * (1.0 / corr_two)
            update = first_next * (1.0 / corr_one) / (scaled * lax.rsqrt(scaled) + epsilon)
            blended = blended_ref[...]
            inner_out[...] = blended - inner_rate * (update + weight_decay * blended)
            first_out[...] = first_next
            second_out[...] = second_next

        step = pl.program_id(0)

        @pl.when(step < A[1] // 2)
        def _():
            store(base_ref[0] + decoded(down_ref[0]) + decoded(across_ref[0]))

        @pl.when(step >= A[1] // 2)
        def _():
            store(base_ref[0] + decoded(down_ref[0]))

    whole = pl.BlockSpec((1, rows, wide), lambda j: (0, 0, j))
    part = pl.BlockSpec((1, rows, wide), lambda j: (0, 0, jnp.minimum(j, A[1] // 2 - 1)))
    state = pl.BlockSpec((rows, wide), lambda j: (0, j))
    out = (jax.ShapeDtypeStruct((rows, width), jnp.float32), state)
    ins = [(base, whole), (down, whole), (across, part)] + [(array, state) for array in states]
    return run(kernel, (width // wide,), ins, [out] * 3, after)


def scatter_blocks(place, inner, places, after=()):
    rows = inner.shape[0]
    n = len(places)

    def kernel(place_ref, *refs):
        for source, target in zip(refs[:n], refs[n:]):
            target[0] = source[...]

    ins = []
    for k in places:
        def source(i, s, k=k):
            return (0, ((s[4] + i) % NH) * NZ + (s[3] + k) % NZ)

        ins.append((inner, pl.BlockSpec((rows, BLOCK), source)))
    out = (
        jax.ShapeDtypeStruct((NH, rows, BLOCK), jnp.float32),
        pl.BlockSpec((1, rows, BLOCK), lambda i, s: (i, 0, 0)),
    )
    return run(kernel, (NH,), ins, [out] * n, after, (place,))


def sum_far(place, inner, arrived, after=()):
    rows = inner.shape[0]

    def kernel(place_ref, own, a, b, c, out):
        out[...] = own[...] + a[0] + b[0] + c[0]

    part = pl.BlockSpec((1, rows, BLOCK), lambda i, s: (1, 0, 0))
    own = pl.BlockSpec((rows, BLOCK), lambda i, s: (0, ((s[4] + 1) % NH) * NZ + s[3]))
    out = (jax.ShapeDtypeStruct((rows, BLOCK), jnp.float32), pl.BlockSpec((rows, BLOCK), lambda i, s: (0, 0)))
    return run(kernel, (1,), [(inner, own)] + [(a, part) for a in arrived], [out], after, (place,))


def outer_step(place, inner, arrived, far, outer_weight, outer_momentum, after=()):
    rows = inner.shape[0]

    def kernel(place_ref, own, a, b, c, far_ref, weight, momentum, next_ref, momentum_ref, code_ref):
        summed = own[...] + a[0] + b[0] + c[0] + far_ref[...]
        average = weight[...] - summed / (NZ * NH)
        momentum_next = outer_decay * momentum[...] + average
        outer_next = weight[...] - outer_rate * (average + outer_decay * momentum_next)
        next_ref[...] = outer_next
        momentum_ref[...] = momentum_next
        code_ref[...] = coded_outer(outer_next)

    part = pl.BlockSpec((1, rows, BLOCK), lambda i, s: (0, 0, 0))
    own = pl.BlockSpec((rows, BLOCK), lambda i, s: (0, s[4] * NZ + s[3]))
    whole = pl.BlockSpec((rows, BLOCK), lambda i, s: (0, 0))
    shape = jax.ShapeDtypeStruct((rows, BLOCK), jnp.float32)
    return run(
        kernel,
        (1,),
        [(inner, own)] + [(a, part) for a in arrived]
        + [(array, whole) for array in (far, outer_weight, outer_momentum)],
        [(shape, whole), (shape, whole), (jax.ShapeDtypeStruct((rows, BLOCK), jnp.bfloat16), whole)],
        after,
        (place,),
    )


def paired(near, far, after=()):
    rows = near.shape[0]

    def kernel(a, b, out):
        out[0] = a[...]
        out[1] = b[...]

    whole = pl.BlockSpec((rows, BLOCK), lambda i: (0, 0))
    out = (
        jax.ShapeDtypeStruct((NH, rows, BLOCK), near.dtype),
        pl.BlockSpec((NH, rows, BLOCK), lambda i: (0, 0, 0)),
    )
    return run(kernel, (1,), [(near, whole), (far, whole)], [out], after)


def blend(place, inner, gathered, buffer=None, after=()):
    rows, width = inner.shape
    n = len(gathered)

    def column(t, s):
        back = gathered[0][0]
        for i, (k, _) in enumerate(gathered):
            back = jnp.where(t // NH == i, k, back)
        return (0, (t % NH + s[4]) % NH * NZ + (s[3] - back + NZ) % NZ)

    def kernel(place_ref, inner_ref, *refs):
        out = refs[-1]
        for i in range(n):

            @pl.when(pl.program_id(0) // NH == i)
            def _():
                out[...] = mix_share * decoded_outer(refs[i][0]) + (1.0 - mix_share) * inner_ref[...]

    code = pl.BlockSpec((1, rows, BLOCK), lambda t, s: (t % NH, 0, 0))
    state = pl.BlockSpec((rows, BLOCK), column)
    ins = [(inner, state)] + [(array, code) for _, array in gathered]
    aliases = {}
    if buffer is not None:
        aliases = {1 + len(ins): 0}
        ins.append((buffer, pl.BlockSpec(memory_space=pl.ANY)))
    out = (jax.ShapeDtypeStruct((rows, width), jnp.float32), state)
    return run(kernel, (NH * n,), ins, [out], after, (place,), aliases=aliases)


def local(
    inner_weight, first_moment, second_moment, outer_weight, outer_momentum, activations, out_grads
):
    inner, first, second = inner_weight[0], first_moment[0], second_moment[0]
    inputs, cotangents = activations[0], out_grads[0]
    replica, member = lax.axis_index("replica"), lax.axis_index("fsdp")
    core, column, row = member % NC, member // NC % NX, member // (NC * NX)
    depth, side = replica % NZ, replica // NZ
    place = jnp.stack([row, column, core, depth, side]).astype(jnp.int32)

    rights = (cotangents, on_fsdp(cotangents, TWIN))
    ahead_one, ahead_three = scatter_blocks(place, inner, (1, 3))
    from_one, from_three = on_replica(ahead_one, AHEAD[1]), on_replica(ahead_three, AHEAD[3])
    far_own, far_send = prepare(place, inputs, 0, 1, (ahead_one,))
    far_left = (far_own, on_fsdp(far_send, TWIN))
    near_own, near_send = prepare(place, inputs, 1, 3, (far_own,))
    near_left = (near_own, on_fsdp(near_send, TWIN))

    across_far_code = product(far_left, rights, (1, 1), B, after=(near_left[1],))
    across_far = on_fsdp(across_far_code, ACROSS)
    up_far_code = product(far_left, rights, (0, 2), A1, after=(across_far_code,))
    up_far = on_fsdp(up_far_code, UP)
    down_far_code = product(far_left, rights, (0, 2), A2, after=(up_far_code,))
    down_far = on_fsdp(down_far_code, DOWN)

    across_near_code = product(near_left, rights, (3, 3), B, after=(down_far_code,))
    across_near = on_fsdp(across_near_code, ACROSS)
    up_own_code = product_pair(
        near_left, rights, 3, A2, far_left, 0, B1[0], across_far, (across_near_code,)
    )
    up_own = on_fsdp(up_own_code, UP)
    ahead_two = scatter_blocks(place, inner, (2,), (up_own_code, from_one, from_three))
    from_two = on_replica(ahead_two, AHEAD[2])

    down_own_code = product_pair(
        near_left, rights, 4, A1, far_left, 0, B2[0], across_far, (ahead_two, up_far)
    )
    down_own = on_fsdp(down_own_code, DOWN)

    up_turn_code = product(
        near_left, rights, (3, 1), A1, ((up_far, 1, (0, 3), 0),), (down_own_code, down_far)
    )
    up_turn = on_fsdp(up_turn_code, UP)

    arrived = (from_one, from_two, from_three)
    far_part = sum_far(place, inner, arrived, (up_turn_code, across_near))
    far_sum = on_replica(far_part, FAR)

    down_turn_code = product(
        near_left, rights, (4, 1), A2, ((down_far, 1, (0, 3), 0),), (far_part, up_own)
    )
    down_turn = on_fsdp(down_turn_code, DOWN)

    outer_next, momentum_next, code = outer_step(
        place, inner, arrived, far_sum, outer_weight, outer_momentum, (down_turn_code, down_own)
    )
    far_code = on_replica(code, FAR)
    up_rest_code = product(
        near_left, rights, (0, 1), ALL,
        ((up_far, 0, A1, 0), (across_near, 0, B, 0), (up_own, 0, B1, A2[1])), (code,),
    )
    up_rest = on_fsdp(up_rest_code, UP)
    down_rest_code = product(
        near_left, rights, (1, 1), ALL,
        ((down_far, 0, A2, 0), (across_near, 1, B, 0), (down_own, 0, B2, A1[1])), (up_rest_code, far_code),
    )
    down_rest = on_fsdp(down_rest_code, DOWN)

    turned_code = product(
        near_left, rights, (5, 1), A,
        ((up_turn, 0, A1, 0), (down_own, 0, A1, 0), (up_own, 0, A2, 0), (down_turn, 0, A2, 0)),
        (down_rest_code,),
    )
    turned = on_fsdp(turned_code, ACROSS)

    pair = paired(code, far_code, (turned_code,))
    from_next, from_last = on_replica(pair, AHEAD[1]), on_replica(pair, AHEAD[3])
    blended = blend(place, inner, [(0, pair)])
    pair_two = paired(code, far_code, (from_next, from_last))
    from_far = on_replica(pair_two, AHEAD[2])
    blended = blend(place, inner, [(1, from_next), (3, from_last)], blended, (pair_two,))
    base = product(
        near_left, rights, (2, 1), ALL, ((across_near, 2, B, 0), (up_rest, 0, ALL, 0)), (blended,),
        jnp.float32,
    )
    blended = blend(place, inner, [(2, from_far)], blended, (base,))
    inner_next, first_next, second_next = finish(base, down_rest, turned, (blended, first, second))
    return (inner_next[None], first_next[None], second_next[None], outer_next, momentum_next)


def solution(mesh):
    in_specs = (
        P("replica", "fsdp", None),
        P("replica", "fsdp", None),
        P("replica", "fsdp", None),
        P("fsdp", "replica"),
        P("fsdp", "replica"),
        P("replica", "fsdp", None),
        P("replica", "fsdp", None),
    )
    out_specs = (
        P("replica", "fsdp", None),
        P("replica", "fsdp", None),
        P("replica", "fsdp", None),
        P("fsdp", "replica"),
        P("fsdp", "replica"),
    )
    return jax.shard_map(local, mesh=mesh, in_specs=in_specs, out_specs=out_specs, check_vma=False)
```

```python
import jax
import jax.numpy as jnp
from jax import lax
from jax.experimental import pallas as pl
from jax.experimental.pallas import tpu as pltpu
from jax.sharding import PartitionSpec as P

outer_rate = 0.7
outer_decay = 0.9
mix_share = 0.5
beta_one = 0.9
beta_two = 0.95
inner_rate = 0.05
weight_decay = 0.1
epsilon = 1e-08
step_count = 200.0
corr_one = 1.0 - beta_one**step_count
corr_two = 1.0 - beta_two**step_count

NY, NX, NC, NZ, NH = 4, 2, 2, 4, 2
BLOCK = 256
A1, A2, B1, B2 = (0, 3), (3, 3), (6, 1), (7, 1)
A, B, ALL = (0, 6), (6, 2), (0, 8)
VMEM = 16 * 2**20


def along_fsdp(move):
    where = [(y, x, c) for y in range(NY) for x in range(NX) for c in range(NC)]
    number = lambda y, x, c: ((y % NY) * NX + x) * NC + c
    return [(number(*place), number(*move(*place))) for place in where]


def along_replica(move):
    where = [(h, z) for h in range(NH) for z in range(NZ)]
    number = lambda h, z: h * NZ + z % NZ
    return [(number(*place), number(*move(*place))) for place in where]


UP = along_fsdp(lambda y, x, c: (y + 1, x, c))
DOWN = along_fsdp(lambda y, x, c: (y - 1, x, c))
ACROSS = along_fsdp(lambda y, x, c: (y, 1 - x, c))
TWIN = along_fsdp(lambda y, x, c: (y, x, 1 - c))
FAR = along_replica(lambda h, z: (1 - h, z))
AHEAD = [along_replica(lambda h, z, k=k: (h, z + k)) for k in range(NZ)]


def on_fsdp(value, pairs):
    return lax.ppermute(value, "fsdp", pairs)


def on_replica(value, pairs):
    return lax.ppermute(value, "replica", pairs)


def coded(value):
    return (value * jnp.abs(value) * (value * value)).astype(jnp.bfloat16)


def decoded(code):
    code = code.astype(jnp.float32)
    root = lax.rsqrt(lax.rsqrt(jnp.abs(code)))
    return jnp.where(code < 0.0, -root, root)


def coded_outer(value):
    value = value * 4096.0
    square = value * value
    fourth = square * square
    return (value * jnp.abs(value) * square * fourth).astype(jnp.bfloat16)


def decoded_outer(code):
    code = code.astype(jnp.float32)
    root = jnp.sqrt(lax.rsqrt(lax.rsqrt(jnp.abs(code)))) * (1.0 / 4096.0)
    return jnp.where(code < 0.0, -root, root)


def run(kernel, grid, ins, outs, after=(), prefetch=(), scratch=(), aliases=None):
    read, late = len(prefetch) + len(ins), len(after)

    def body(*refs):
        kernel(*refs[:read], *refs[read + late :])

    arrays = [array for array, _ in ins]
    shapes = tuple(shape for shape, _ in outs)
    result = pl.pallas_call(
        body,
        out_shape=shapes,
        grid_spec=pltpu.PrefetchScalarGridSpec(
            num_scalar_prefetch=len(prefetch),
            grid=grid,
            in_specs=[spec for _, spec in ins] + [pl.BlockSpec(memory_space=pl.ANY)] * late,
            out_specs=tuple(spec for _, spec in outs),
            scratch_shapes=list(scratch),
        ),
        input_output_aliases=aliases or {},
        compiler_params=pltpu.CompilerParams(vmem_limit_bytes=VMEM),
        cost_estimate=pl.CostEstimate(flops=1, bytes_accessed=1, transcendentals=0),
    )(*prefetch, *arrays, *after)
    return result[0] if len(outs) == 1 else result


def prepare(place, activations, first, count, after=()):
    tokens, width = activations.shape
    quarter = width // NY
    rows = quarter // (NX * NC)

    def distance(i):
        step = first + i
        return jnp.where(step == 0, 2, jnp.where(step == 1, 1, jnp.where(step == 2, 3, 0)))

    def kernel(place_ref, a_ref, own_ref, send_ref, turned):
        turned[...] = a_ref[...].T
        x, core = place_ref[1], place_ref[2]
        for dx in range(NX):
            column = (x + dx) % NX
            own = pl.multiple_of((column * NC + core) * rows, 16)
            other = pl.multiple_of((column * NC + 1 - core) * rows, 16)
            own_ref[dx, 0] = turned[pl.ds(own, rows), :]
            send_ref[dx, 0] = turned[pl.ds(other, rows), :]

    out = (
        jax.ShapeDtypeStruct((NX, count, rows, tokens), jnp.bfloat16),
        pl.BlockSpec((NX, 1, rows, tokens), lambda i, s: (0, i, 0, 0)),
    )
    source = pl.BlockSpec((tokens, quarter), lambda i, s: (0, (s[0] + distance(i)) % NY))
    own, send = run(
        kernel, (count,), [(activations, source)], [out, out], after, (place,),
        [pltpu.VMEM((quarter, tokens), jnp.bfloat16)],
    )
    return own.reshape(NX * count, rows, tokens), send.reshape(NX * count, rows, tokens)


def run_whole(kernel, arrays, shape, after=()):
    count = len(arrays)
    vmem = pl.BlockSpec(memory_space=pltpu.VMEM)

    def body(*refs):
        kernel(*refs[:count], *refs[count + len(after) :])

    return pl.pallas_call(
        body,
        out_shape=shape,
        in_specs=[vmem] * count + [pl.BlockSpec(memory_space=pl.ANY)] * len(after),
        out_specs=jax.tree.map(lambda _: vmem, shape),
        compiler_params=pltpu.CompilerParams(vmem_limit_bytes=VMEM),
    )(*arrays, *after)


def block_columns(j):
    start = j * BLOCK
    return pl.ds(start if isinstance(start, int) else pl.multiple_of(start, BLOCK), BLOCK)


def dots(lefts, rights, blocks, j):
    start, count = blocks
    total = None
    for left, right in zip(lefts, rights):
        rows, depth = left.shape[1:]
        part = left[start : start + count].reshape(count * rows, depth)
        part = jnp.dot(part, right[:, block_columns(j)], preferred_element_type=jnp.float32)
        total = part if total is None else total + part
    return total.reshape(count, rows, BLOCK)


def regions(number, received):
    cuts = {0, number}
    for _, _, span, _ in received:
        cuts |= {span[0], span[0] + span[1]}
    cuts = sorted(cuts)
    found = []
    for low, high in zip(cuts, cuts[1:]):
        which = [i for i, (_, _, span, _) in enumerate(received) if span[0] <= low < span[0] + span[1]]
        found.append((low, high, which))
    return found


def product(lefts, rights, blocks, columns, received=(), after=(), kind=jnp.bfloat16):
    first, number = columns
    count, rows = blocks[1], lefts[0].shape[1]

    def kernel(lo, lt, ro, rt, *rest):
        out = rest[-1]

        def step(j, which):
            total = dots((lo, lt), (ro, rt), blocks, first + j)
            for i in which:
                _, block, span, offset = received[i]
                total = total + decoded(rest[i][block : block + count, :, block_columns(offset + j - span[0])])
            out[:, :, block_columns(j)] = coded(total) if kind == jnp.bfloat16 else total

        for low, high, which in regions(number, received):
            pl.loop(low, high)(lambda j, which=which: step(j, which))

    shape = jax.ShapeDtypeStruct((count, rows, number * BLOCK), kind)
    return run_whole(kernel, [*lefts, *rights, *(array for array, *_ in received)], shape, after)


def combined(partial, block, columns, received, after=()):
    first, number = columns
    rows = partial.shape[1]

    def kernel(values, *rest):
        out = rest[-1]

        def step(j, which):
            total = values[block : block + 1, :, block_columns(first + j)]
            for i in which:
                _, row, span, offset = received[i]
                total = total + decoded(rest[i][row : row + 1, :, block_columns(offset + j - span[0])])
            out[:, :, block_columns(j)] = coded(total)

        for low, high, which in regions(number, received):
            pl.loop(low, high)(lambda j, which=which: step(j, which))

    shape = jax.ShapeDtypeStruct((1, rows, number * BLOCK), jnp.bfloat16)
    return run_whole(kernel, [partial, *(array for array, *_ in received)], shape, after)


def product_pair(lefts, rights, block, columns, lefts_last, block_last, columns_last, codes, after=()):
    first, number = columns
    first_last, number_last = columns_last
    rows = lefts[0].shape[1]

    def kernel(lo, lt, lo2, lt2, ro, rt, code, out):
        @pl.loop(0, number)
        def _(j):
            out[:, :, block_columns(j)] = coded(dots((lo, lt), (ro, rt), (block, 1), first + j))

        @pl.loop(0, number_last)
        def _(j):
            total = dots((lo2, lt2), (ro, rt), (block_last, 1), first_last + j)
            total = total + decoded(code[:, :, block_columns(first_last - B[0] + j)])
            out[:, :, block_columns(number + j)] = coded(total)

    shape = jax.ShapeDtypeStruct((1, rows, (number + number_last) * BLOCK), jnp.bfloat16)
    return run_whole(kernel, [*lefts, *lefts_last, *rights, codes], shape, after)


def prepare_finish(partial, block, received, up, first, second, after=()):
    rows = partial.shape[1]

    def kernel(values, code, up_ref, first_ref, second_ref, base, first_out, second_out):
        def step(j, with_code):
            columns = block_columns(j)
            total = values[block, :, columns] + decoded(up_ref[0, :, columns])
            if with_code:
                total = total + decoded(code[received[1], :, block_columns(j - B[0])])
            base[:, columns] = total
            first_out[:, columns] = beta_one * first_ref[:, columns] + (1.0 - beta_one) * total
            second_out[:, columns] = beta_two * second_ref[:, columns]

        pl.loop(0, B[0])(lambda j: step(j, False))
        pl.loop(B[0], ALL[1])(lambda j: step(j, True))

    shape = (jax.ShapeDtypeStruct((rows, ALL[1] * BLOCK), jnp.float32),) * 3
    return run_whole(kernel, [partial, received[0], up, first, second], shape, after)


def finish(base, first_part, second_part, blended, down, across, after=()):
    rows, width = base.shape
    wide = 2 * BLOCK
    cut = A[1] // 2

    def kernel(base_ref, first_ref, second_ref, blended_ref, down_ref, across_ref, inner_out, first_out, second_out):
        def store(rest):
            total = base_ref[...] + rest
            first_next = first_ref[...] + (1.0 - beta_one) * rest
            second_next = second_ref[...] + (1.0 - beta_two) * total * total
            scaled = second_next * (1.0 / corr_two)
            update = first_next * (1.0 / corr_one) / (scaled * lax.rsqrt(scaled) + epsilon)
            blended = blended_ref[...]
            inner_out[...] = blended - inner_rate * (update + weight_decay * blended)
            first_out[...] = first_next
            second_out[...] = second_next

        step = pl.program_id(0)

        @pl.when(step < cut)
        def _():
            store(decoded(down_ref[0]) + decoded(across_ref[0]))

        @pl.when(step >= cut)
        def _():
            store(decoded(down_ref[0]))

    whole = pl.BlockSpec((1, rows, wide), lambda j: (0, 0, j))
    part = pl.BlockSpec((1, rows, wide), lambda j: (0, 0, jnp.minimum(j, cut - 1)))
    state = pl.BlockSpec((rows, wide), lambda j: (0, j))
    out = (jax.ShapeDtypeStruct((rows, width), jnp.float32), state)
    ins = [(array, state) for array in (base, first_part, second_part, blended)]
    ins += [(down, whole), (across, part)]
    return run(kernel, (width // wide,), ins, [out] * 3, after)


def scatter_blocks(place, inner, places, after=()):
    rows = inner.shape[0]
    n = len(places)

    def kernel(place_ref, *refs):
        for source, target in zip(refs[:n], refs[n:]):
            target[0] = source[...]

    ins = []
    for k in places:
        def source(i, s, k=k):
            return (0, ((s[4] + i) % NH) * NZ + (s[3] + k) % NZ)

        ins.append((inner, pl.BlockSpec((rows, BLOCK), source)))
    out = (
        jax.ShapeDtypeStruct((NH, rows, BLOCK), jnp.float32),
        pl.BlockSpec((1, rows, BLOCK), lambda i, s: (i, 0, 0)),
    )
    return run(kernel, (NH,), ins, [out] * n, after, (place,))


outer_share = 1.0 - outer_rate * (1.0 + outer_decay)
sum_share = outer_rate * (1.0 + outer_decay) / (NZ * NH)
momentum_share = -outer_rate * outer_decay * outer_decay


def sum_line(place, inner, arrived, outer_weight, outer_momentum, after=()):
    rows = inner.shape[0]

    def kernel(place_ref, near, far, *rest):
        here, there, weight, momentum, out = rest[:3], rest[3:6], rest[6], rest[7], rest[8]
        out[0] = far[...] + there[0][0] + there[1][0] + there[2][0]
        summed = near[...] + here[0][0] + here[1][0] + here[2][0]
        out[1] = outer_share * weight[...] + momentum_share * momentum[...] + sum_share * summed

    def own(d):
        return pl.BlockSpec((rows, BLOCK), lambda i, s: (0, ((s[4] + d) % NH) * NZ + s[3]))

    def part(d):
        return pl.BlockSpec((1, rows, BLOCK), lambda i, s: (d, 0, 0))

    whole = pl.BlockSpec((rows, BLOCK), lambda i, s: (0, 0))
    ins = [(inner, own(0)), (inner, own(1))]
    ins += [(a, part(0)) for a in arrived] + [(a, part(1)) for a in arrived]
    ins += [(outer_weight, whole), (outer_momentum, whole)]
    out = (
        jax.ShapeDtypeStruct((NH, rows, BLOCK), jnp.float32),
        pl.BlockSpec((NH, rows, BLOCK), lambda i, s: (0, 0, 0)),
    )
    return run(kernel, (1,), ins, [out], after, (place,))


def outer_step(place, inner, arrived, line, far, outer_weight, outer_momentum, after=()):
    rows = inner.shape[0]

    def kernel(place_ref, own, a, b, c, line_ref, far_ref, weight, momentum, next_ref, momentum_ref, code_ref):
        summed = own[...] + a[0] + b[0] + c[0] + far_ref[0]
        average = weight[...] - summed / (NZ * NH)
        momentum_next = outer_decay * momentum[...] + average
        outer_next = weight[...] - outer_rate * (average + outer_decay * momentum_next)
        next_ref[...] = outer_next
        momentum_ref[...] = momentum_next
        code_ref[0] = coded_outer(outer_next)
        code_ref[1] = coded_outer(far_ref[1] + sum_share * line_ref[0])

    part = pl.BlockSpec((1, rows, BLOCK), lambda i, s: (0, 0, 0))
    both = pl.BlockSpec((NH, rows, BLOCK), lambda i, s: (0, 0, 0))
    own = pl.BlockSpec((rows, BLOCK), lambda i, s: (0, s[4] * NZ + s[3]))
    whole = pl.BlockSpec((rows, BLOCK), lambda i, s: (0, 0))
    shape = jax.ShapeDtypeStruct((rows, BLOCK), jnp.float32)
    return run(
        kernel,
        (1,),
        [(inner, own)] + [(a, part) for a in arrived]
        + [(line, part), (far, both), (outer_weight, whole), (outer_momentum, whole)],
        [(shape, whole), (shape, whole), (jax.ShapeDtypeStruct((NH, rows, BLOCK), jnp.bfloat16), both)],
        after,
        (place,),
    )


def copied(array, after=()):
    def kernel(source, out):
        out[...] = source[...]

    return run_whole(kernel, [array], jax.ShapeDtypeStruct(array.shape, array.dtype), after)


def blend(place, inner, gathered, buffer=None, after=()):
    rows, width = inner.shape
    n = len(gathered)
    held = [i for i in range(n) if gathered[i][1] is not None]
    known = {i: place for place, i in enumerate(held)}

    def column(t, s):
        back = gathered[0][0]
        for i, (k, _) in enumerate(gathered):
            back = jnp.where(t // NH == i, k, back)
        return (0, (t % NH + s[4]) % NH * NZ + (s[3] - back + NZ) % NZ)

    def kernel(place_ref, inner_ref, *refs):
        out = refs[-1]
        for i in range(n):

            @pl.when(pl.program_id(0) // NH == i)
            def _():
                half = (1.0 - mix_share) * inner_ref[...]
                if gathered[i][1] is not None:
                    half = mix_share * decoded_outer(refs[known[i]][0]) + half
                out[...] = half

    code = pl.BlockSpec((1, rows, BLOCK), lambda t, s: (t % NH, 0, 0))
    state = pl.BlockSpec((rows, BLOCK), column)
    ins = [(inner, state)] + [(gathered[i][1], code) for i in held]
    aliases = {}
    if buffer is not None:
        aliases = {1 + len(ins): 0}
        ins.append((buffer, pl.BlockSpec(memory_space=pl.ANY)))
    out = (jax.ShapeDtypeStruct((rows, width), jnp.float32), state)
    return run(kernel, (NH * n,), ins, [out], after, (place,), aliases=aliases)


def local(
    inner_weight, first_moment, second_moment, outer_weight, outer_momentum, activations, out_grads
):
    inner, first, second = inner_weight[0], first_moment[0], second_moment[0]
    inputs, cotangents = activations[0], out_grads[0]
    replica, member = lax.axis_index("replica"), lax.axis_index("fsdp")
    core, column, row = member % NC, member // NC % NX, member // (NC * NX)
    depth, side = replica % NZ, replica // NZ
    place = jnp.stack([row, column, core, depth, side]).astype(jnp.int32)

    rights = (cotangents, on_fsdp(cotangents, TWIN))
    ahead_one, ahead_three = scatter_blocks(place, inner, (1, 3))
    from_one, from_three = on_replica(ahead_one, AHEAD[1]), on_replica(ahead_three, AHEAD[3])
    far_own, far_send = prepare(place, inputs, 0, 1, (ahead_one,))
    far_left = (far_own, on_fsdp(far_send, TWIN))
    near_own, near_send = prepare(place, inputs, 1, 3, (far_own,))
    near_left = (near_own, on_fsdp(near_send, TWIN))

    across_far_code = product(far_left, rights, (1, 1), B, after=(near_left[1],))
    across_far = on_fsdp(across_far_code, ACROSS)
    up_far_code = product(far_left, rights, (0, 2), A1, after=(across_far_code,))
    up_far = on_fsdp(up_far_code, UP)
    down_far_code = product(far_left, rights, (0, 2), A2, after=(up_far_code,))
    down_far = on_fsdp(down_far_code, DOWN)

    across_near_code = product(near_left, rights, (3, 3), B, after=(down_far_code,))
    across_near = on_fsdp(across_near_code, ACROSS)
    up_own_code = product_pair(
        near_left, rights, 3, A2, far_left, 0, B1, across_far, (across_near_code,)
    )
    up_own = on_fsdp(up_own_code, UP)
    ahead_two = scatter_blocks(place, inner, (2,), (up_own_code, from_one, from_three))
    from_two = on_replica(ahead_two, AHEAD[2])

    partial = product(near_left, rights, (0, 3), ALL, after=(ahead_two,), kind=jnp.float32)
    partial_turn = product(near_left, rights, (5, 1), A, after=(partial,), kind=jnp.float32)

    down_own_code = product_pair(
        near_left, rights, 4, A1, far_left, 0, B2, across_far, (partial_turn, up_far)
    )
    down_own = on_fsdp(down_own_code, DOWN)

    up_turn_code = product(
        near_left, rights, (3, 1), A1, ((up_far, 1, A1, 0),), (down_own_code, down_far)
    )
    up_turn = on_fsdp(up_turn_code, UP)

    arrived = (from_one, from_two, from_three)
    line = sum_line(
        place, inner, arrived, outer_weight, outer_momentum, (up_turn_code, across_near)
    )
    far_line = on_replica(line, FAR)

    down_turn_code = product(
        near_left, rights, (4, 1), A2, ((down_far, 1, (0, A2[1]), 0),), (line, up_own)
    )
    down_turn = on_fsdp(down_turn_code, DOWN)

    up_rest_code = combined(
        partial, 0, ALL,
        ((up_far, 0, A1, 0), (across_near, 0, B, 0), (up_own, 0, B1, A2[1])), (down_turn_code,),
    )
    up_rest = on_fsdp(up_rest_code, UP)
    down_rest_code = combined(
        partial, 1, ALL,
        ((down_far, 0, A2, 0), (across_near, 1, B, 0), (down_own, 0, B2, A1[1])), (up_rest_code,),
    )
    down_rest = on_fsdp(down_rest_code, DOWN)

    outer_next, momentum_next, pair = outer_step(
        place, inner, arrived, line, far_line, outer_weight, outer_momentum, (down_rest_code, up_turn)
    )
    turned_code = combined(
        partial_turn, 0, A,
        ((up_turn, 0, A1, 0), (down_own, 0, A1, 0), (up_own, 0, A2, 0), (down_turn, 0, A2, 0)),
        (pair,),
    )
    turned = on_fsdp(turned_code, ACROSS)

    from_next, from_last = on_replica(pair, AHEAD[1]), on_replica(pair, AHEAD[3])
    blended = blend(place, inner, [(0, pair)], None, (turned_code,))
    pair_two = copied(pair, (blended, from_next, from_last))
    from_far = on_replica(pair_two, AHEAD[2])
    blended = blend(place, inner, [(3, from_last), (1, from_next)], blended, (pair_two,))
    base, first_part, second_part = prepare_finish(
        partial, 2, (across_near, 2), up_rest, first, second, (blended,)
    )
    blended = blend(place, inner, [(2, from_far)], blended, (base,))
    inner_next, first_next, second_next = finish(
        base, first_part, second_part, blended, down_rest, turned
    )
    return (inner_next[None], first_next[None], second_next[None], outer_next, momentum_next)


def solution(mesh):
    in_specs = (
        P("replica", "fsdp", None),
        P("replica", "fsdp", None),
        P("replica", "fsdp", None),
        P("fsdp", "replica"),
        P("fsdp", "replica"),
        P("replica", "fsdp", None),
        P("replica", "fsdp", None),
    )
    out_specs = (
        P("replica", "fsdp", None),
        P("replica", "fsdp", None),
        P("replica", "fsdp", None),
        P("fsdp", "replica"),
        P("fsdp", "replica"),
    )
    return jax.shard_map(local, mesh=mesh, in_specs=in_specs, out_specs=out_specs, check_vma=False)
```

```python
import jax
import jax.numpy as jnp
from jax import lax
from jax.experimental import pallas as pl
from jax.experimental.pallas import tpu as pltpu
from jax.sharding import PartitionSpec as P

outer_rate = 0.7
outer_decay = 0.9
mix_share = 0.5
beta_one = 0.9
beta_two = 0.95
inner_rate = 0.05
weight_decay = 0.1
epsilon = 1e-08
step_count = 200.0
corr_one = 1.0 - beta_one**step_count
corr_two = 1.0 - beta_two**step_count

NY, NX, NC, NZ, NH = 4, 2, 2, 4, 2
BLOCK = 256
A1, A2, B1, B2 = (0, 3), (3, 3), (6, 1), (7, 1)
A, B, ALL = (0, 6), (6, 2), (0, 8)
VMEM = 16 * 2**20


def along_fsdp(move):
    where = [(y, x, c) for y in range(NY) for x in range(NX) for c in range(NC)]
    number = lambda y, x, c: ((y % NY) * NX + x) * NC + c
    return [(number(*place), number(*move(*place))) for place in where]


def along_replica(move):
    where = [(h, z) for h in range(NH) for z in range(NZ)]
    number = lambda h, z: h * NZ + z % NZ
    return [(number(*place), number(*move(*place))) for place in where]


UP = along_fsdp(lambda y, x, c: (y + 1, x, c))
DOWN = along_fsdp(lambda y, x, c: (y - 1, x, c))
ACROSS = along_fsdp(lambda y, x, c: (y, 1 - x, c))
TWIN = along_fsdp(lambda y, x, c: (y, x, 1 - c))
FAR = along_replica(lambda h, z: (1 - h, z))
AHEAD = [along_replica(lambda h, z, k=k: (h, z + k)) for k in range(NZ)]


def on_fsdp(value, pairs):
    return lax.ppermute(value, "fsdp", pairs)


def on_replica(value, pairs):
    return lax.ppermute(value, "replica", pairs)


def coded(value):
    return (value * jnp.abs(value) * (value * value)).astype(jnp.bfloat16)


def decoded(code):
    code = code.astype(jnp.float32)
    root = lax.rsqrt(lax.rsqrt(jnp.abs(code)))
    return jnp.where(code < 0.0, -root, root)


def coded_outer(value):
    value = value * 4096.0
    square = value * value
    fourth = square * square
    return (value * jnp.abs(value) * square * fourth).astype(jnp.bfloat16)


def decoded_outer(code):
    code = code.astype(jnp.float32)
    root = jnp.sqrt(lax.rsqrt(lax.rsqrt(jnp.abs(code)))) * (1.0 / 4096.0)
    return jnp.where(code < 0.0, -root, root)


def run(kernel, grid, ins, outs, after=(), prefetch=(), scratch=(), aliases=None):
    read, late = len(prefetch) + len(ins), len(after)

    def body(*refs):
        kernel(*refs[:read], *refs[read + late :])

    arrays = [array for array, _ in ins]
    shapes = tuple(shape for shape, _ in outs)
    result = pl.pallas_call(
        body,
        out_shape=shapes,
        grid_spec=pltpu.PrefetchScalarGridSpec(
            num_scalar_prefetch=len(prefetch),
            grid=grid,
            in_specs=[spec for _, spec in ins] + [pl.BlockSpec(memory_space=pl.ANY)] * late,
            out_specs=tuple(spec for _, spec in outs),
            scratch_shapes=list(scratch),
        ),
        input_output_aliases=aliases or {},
        compiler_params=pltpu.CompilerParams(vmem_limit_bytes=VMEM),
        cost_estimate=pl.CostEstimate(flops=1, bytes_accessed=1, transcendentals=0),
    )(*prefetch, *arrays, *after)
    return result[0] if len(outs) == 1 else result


def prepare(place, activations, after=()):
    tokens, width = activations.shape
    quarter = width // NY
    rows = quarter // (NX * NC)

    def distance(i):
        return jnp.where(i == 0, 2, jnp.where(i == 1, 1, jnp.where(i == 2, 3, 0)))

    def kernel(place_ref, a_ref, far_own, far_send, near_own, near_send, turned):
        turned[...] = a_ref[...].T
        x, core = place_ref[1], place_ref[2]

        def write(own_ref, send_ref):
            for dx in range(NX):
                column = (x + dx) % NX
                own = pl.multiple_of((column * NC + core) * rows, 16)
                other = pl.multiple_of((column * NC + 1 - core) * rows, 16)
                own_ref[dx, 0] = turned[pl.ds(own, rows), :]
                send_ref[dx, 0] = turned[pl.ds(other, rows), :]

        pl.when(pl.program_id(0) == 0)(lambda: write(far_own, far_send))
        pl.when(pl.program_id(0) > 0)(lambda: write(near_own, near_send))

    def out(count):
        return (
            jax.ShapeDtypeStruct((NX, count, rows, tokens), jnp.bfloat16),
            pl.BlockSpec((NX, 1, rows, tokens), lambda i, s: (0, 0 if count == 1 else jnp.maximum(i - 1, 0), 0, 0)),
        )

    source = pl.BlockSpec((tokens, quarter), lambda i, s: (0, (s[0] + distance(i)) % NY))
    results = run(
        kernel, (NY,), [(activations, source)], [out(1), out(1), out(NY - 1), out(NY - 1)], after, (place,),
        [pltpu.VMEM((quarter, tokens), jnp.bfloat16)],
    )
    return [array.reshape(-1, rows, tokens) for array in results]


def run_whole(kernel, arrays, shape, after=()):
    count = len(arrays)
    vmem = pl.BlockSpec(memory_space=pltpu.VMEM)

    def body(*refs):
        kernel(*refs[:count], *refs[count + len(after) :])

    return pl.pallas_call(
        body,
        out_shape=shape,
        in_specs=[vmem] * count + [pl.BlockSpec(memory_space=pl.ANY)] * len(after),
        out_specs=jax.tree.map(lambda _: vmem, shape),
        compiler_params=pltpu.CompilerParams(vmem_limit_bytes=VMEM),
    )(*arrays, *after)


def block_columns(j):
    start = j * BLOCK
    return pl.ds(start if isinstance(start, int) else pl.multiple_of(start, BLOCK), BLOCK)


def dots(lefts, rights, blocks, j):
    start, count = blocks
    total = None
    for left, right in zip(lefts, rights):
        rows, depth = left.shape[1:]
        part = left[start : start + count].reshape(count * rows, depth)
        part = jnp.dot(part, right[:, block_columns(j)], preferred_element_type=jnp.float32)
        total = part if total is None else total + part
    return total.reshape(count, rows, BLOCK)


def regions(number, received):
    cuts = {0, number}
    for _, _, span, _ in received:
        cuts |= {span[0], span[0] + span[1]}
    cuts = sorted(cuts)
    found = []
    for low, high in zip(cuts, cuts[1:]):
        which = [i for i, (_, _, span, _) in enumerate(received) if span[0] <= low < span[0] + span[1]]
        found.append((low, high, which))
    return found


def product(lefts, rights, blocks, columns, received=(), after=(), kind=jnp.bfloat16):
    first, number = columns
    count, rows = blocks[1], lefts[0].shape[1]

    def kernel(lo, lt, ro, rt, *rest):
        out = rest[-1]

        def step(j, which):
            total = dots((lo, lt), (ro, rt), blocks, first + j)
            for i in which:
                _, block, span, offset = received[i]
                total = total + decoded(rest[i][block : block + count, :, block_columns(offset + j - span[0])])
            out[:, :, block_columns(j)] = coded(total) if kind == jnp.bfloat16 else total

        for low, high, which in regions(number, received):
            pl.loop(low, high)(lambda j, which=which: step(j, which))

    shape = jax.ShapeDtypeStruct((count, rows, number * BLOCK), kind)
    return run_whole(kernel, [*lefts, *rights, *(array for array, *_ in received)], shape, after)


def combined(partial, block, columns, received, after=()):
    first, number = columns
    rows = partial.shape[1]

    def kernel(values, *rest):
        out = rest[-1]

        def step(j, which):
            total = values[block : block + 1, :, block_columns(first + j)]
            for i in which:
                _, row, span, offset = received[i]
                total = total + decoded(rest[i][row : row + 1, :, block_columns(offset + j - span[0])])
            out[:, :, block_columns(j)] = coded(total)

        for low, high, which in regions(number, received):
            pl.loop(low, high)(lambda j, which=which: step(j, which))

    shape = jax.ShapeDtypeStruct((1, rows, number * BLOCK), jnp.bfloat16)
    return run_whole(kernel, [partial, *(array for array, *_ in received)], shape, after)


def product_pair(lefts, rights, block, columns, lefts_last, block_last, columns_last, codes, after=()):
    first, number = columns
    first_last, number_last = columns_last
    rows = lefts[0].shape[1]

    def kernel(lo, lt, lo2, lt2, ro, rt, code, out):
        @pl.loop(0, number)
        def _(j):
            out[:, :, block_columns(j)] = coded(dots((lo, lt), (ro, rt), (block, 1), first + j))

        @pl.loop(0, number_last)
        def _(j):
            total = dots((lo2, lt2), (ro, rt), (block_last, 1), first_last + j)
            total = total + decoded(code[:, :, block_columns(first_last - B[0] + j)])
            out[:, :, block_columns(number + j)] = coded(total)

    shape = jax.ShapeDtypeStruct((1, rows, (number + number_last) * BLOCK), jnp.bfloat16)
    return run_whole(kernel, [*lefts, *lefts_last, *rights, codes], shape, after)


def prepare_finish(partial, block, received, up, first, second, after=()):
    rows = partial.shape[1]

    def kernel(values, code, up_ref, first_ref, second_ref, base, first_out, second_out):
        def step(j, with_code):
            columns = block_columns(j)
            total = values[block, :, columns] + decoded(up_ref[0, :, columns])
            if with_code:
                total = total + decoded(code[received[1], :, block_columns(j - B[0])])
            base[:, columns] = total
            first_out[:, columns] = beta_one * first_ref[:, columns] + (1.0 - beta_one) * total
            second_out[:, columns] = beta_two * second_ref[:, columns]

        pl.loop(0, B[0])(lambda j: step(j, False))
        pl.loop(B[0], ALL[1])(lambda j: step(j, True))

    shape = (jax.ShapeDtypeStruct((rows, ALL[1] * BLOCK), jnp.float32),) * 3
    return run_whole(kernel, [partial, received[0], up, first, second], shape, after)


def finish(base, first_part, second_part, blended, down, across, after=()):
    rows, width = base.shape
    wide = 2 * BLOCK
    cut = A[1] // 2

    def kernel(base_ref, first_ref, second_ref, blended_ref, down_ref, across_ref, inner_out, first_out, second_out):
        def store(rest):
            total = base_ref[...] + rest
            first_next = first_ref[...] + (1.0 - beta_one) * rest
            second_next = second_ref[...] + (1.0 - beta_two) * total * total
            scaled = second_next * (1.0 / corr_two)
            update = first_next * (1.0 / corr_one) / (scaled * lax.rsqrt(scaled) + epsilon)
            blended = blended_ref[...]
            inner_out[...] = blended - inner_rate * (update + weight_decay * blended)
            first_out[...] = first_next
            second_out[...] = second_next

        step = pl.program_id(0)

        @pl.when(step < cut)
        def _():
            store(decoded(down_ref[0]) + decoded(across_ref[0]))

        @pl.when(step >= cut)
        def _():
            store(decoded(down_ref[0]))

    whole = pl.BlockSpec((1, rows, wide), lambda j: (0, 0, j))
    part = pl.BlockSpec((1, rows, wide), lambda j: (0, 0, jnp.minimum(j, cut - 1)))
    state = pl.BlockSpec((rows, wide), lambda j: (0, j))
    out = (jax.ShapeDtypeStruct((rows, width), jnp.float32), state)
    ins = [(array, state) for array in (base, first_part, second_part, blended)]
    ins += [(down, whole), (across, part)]
    return run(kernel, (width // wide,), ins, [out] * 3, after)


def scatter_blocks(place, inner, places, after=()):
    rows = inner.shape[0]
    n = len(places)

    def kernel(place_ref, *refs):
        for source, target in zip(refs[:n], refs[n:]):
            target[0] = source[...]

    ins = []
    for k in places:
        def source(i, s, k=k):
            return (0, ((s[4] + i) % NH) * NZ + (s[3] + k) % NZ)

        ins.append((inner, pl.BlockSpec((rows, BLOCK), source)))
    out = (
        jax.ShapeDtypeStruct((NH, rows, BLOCK), jnp.float32),
        pl.BlockSpec((1, rows, BLOCK), lambda i, s: (i, 0, 0)),
    )
    return run(kernel, (NH,), ins, [out] * n, after, (place,))


outer_share = 1.0 - outer_rate * (1.0 + outer_decay)
sum_share = outer_rate * (1.0 + outer_decay) / (NZ * NH)
momentum_share = -outer_rate * outer_decay * outer_decay


def sum_line(place, inner, arrived, outer_weight, outer_momentum, after=()):
    rows = inner.shape[0]

    def kernel(place_ref, near, far, *rest):
        here, there, weight, momentum, sum_out, out = rest[:3], rest[3:6], rest[6], rest[7], rest[8], rest[9]
        out[0] = far[...] + there[0][0] + there[1][0] + there[2][0]
        summed = near[...] + here[0][0] + here[1][0] + here[2][0]
        sum_out[...] = summed
        out[1] = outer_share * weight[...] + momentum_share * momentum[...] + sum_share * summed

    def own(d):
        return pl.BlockSpec((rows, BLOCK), lambda i, s: (0, ((s[4] + d) % NH) * NZ + s[3]))

    def part(d):
        return pl.BlockSpec((1, rows, BLOCK), lambda i, s: (d, 0, 0))

    whole = pl.BlockSpec((rows, BLOCK), lambda i, s: (0, 0))
    ins = [(inner, own(0)), (inner, own(1))]
    ins += [(a, part(0)) for a in arrived] + [(a, part(1)) for a in arrived]
    ins += [(outer_weight, whole), (outer_momentum, whole)]
    outs = [
        (jax.ShapeDtypeStruct((rows, BLOCK), jnp.float32), whole),
        (
            jax.ShapeDtypeStruct((NH, rows, BLOCK), jnp.float32),
            pl.BlockSpec((NH, rows, BLOCK), lambda i, s: (0, 0, 0)),
        ),
    ]
    return run(kernel, (1,), ins, outs, after, (place,))


def outer_step(line_sum, line, far, outer_weight, outer_momentum, after=()):
    def kernel(sum_ref, line_ref, far_ref, weight, momentum, next_ref, momentum_ref, code_ref):
        average = weight[...] - (sum_ref[...] + far_ref[0]) / (NZ * NH)
        momentum_next = outer_decay * momentum[...] + average
        outer_next = weight[...] - outer_rate * (average + outer_decay * momentum_next)
        next_ref[...] = outer_next
        momentum_ref[...] = momentum_next
        code_ref[0] = coded_outer(outer_next)
        code_ref[1] = coded_outer(far_ref[1] + sum_share * line_ref[0])

    shape = jax.ShapeDtypeStruct(line_sum.shape, jnp.float32)
    shapes = (shape, shape, jax.ShapeDtypeStruct(line.shape, jnp.bfloat16))
    return run_whole(kernel, [line_sum, line, far, outer_weight, outer_momentum], shapes, after)


def copied(array, after=()):
    def kernel(source, out):
        out[...] = source[...]

    return run_whole(kernel, [array], jax.ShapeDtypeStruct(array.shape, array.dtype), after)


def blend(place, inner, gathered, buffer=None, after=()):
    count = len(gathered)

    def kernel(place_ref, inner_ref, *rest):
        out = rest[-1]
        for (back, _), code in zip(gathered, rest):
            for d in range(NH):
                column = (d + place_ref[4]) % NH * NZ + (place_ref[3] - back + NZ) % NZ
                half = (1.0 - mix_share) * inner_ref[:, block_columns(column)]
                out[:, block_columns(column)] = mix_share * decoded_outer(code[d]) + half

    vmem = pl.BlockSpec(memory_space=pltpu.VMEM)
    operands = [place, inner, *(codes for _, codes in gathered)]
    specs = [pl.BlockSpec(memory_space=pltpu.SMEM)] + [vmem] * (1 + count)
    aliases = {}
    if buffer is not None:
        aliases = {len(operands): 0}
        operands.append(buffer)
        specs.append(vmem)
    return pl.pallas_call(
        kernel,
        out_shape=jax.ShapeDtypeStruct(inner.shape, jnp.float32),
        in_specs=specs + [pl.BlockSpec(memory_space=pl.ANY)] * len(after),
        out_specs=vmem,
        input_output_aliases=aliases,
        compiler_params=pltpu.CompilerParams(vmem_limit_bytes=VMEM),
    )(*operands, *after)


def local(
    inner_weight, first_moment, second_moment, outer_weight, outer_momentum, activations, out_grads
):
    inner, first, second = inner_weight[0], first_moment[0], second_moment[0]
    inputs, cotangents = activations[0], out_grads[0]
    replica, member = lax.axis_index("replica"), lax.axis_index("fsdp")
    core, column, row = member % NC, member // NC % NX, member // (NC * NX)
    depth, side = replica % NZ, replica // NZ
    place = jnp.stack([row, column, core, depth, side]).astype(jnp.int32)

    rights = (cotangents, on_fsdp(cotangents, TWIN))
    far_own, far_send, near_own, near_send = prepare(place, inputs)
    far_left = (far_own, on_fsdp(far_send, TWIN))
    near_left = (near_own, on_fsdp(near_send, TWIN))
    ahead_one, ahead_three = scatter_blocks(place, inner, (1, 3), (far_own,))
    from_one, from_three = on_replica(ahead_one, AHEAD[1]), on_replica(ahead_three, AHEAD[3])

    across_far_code = product(far_left, rights, (1, 1), B, after=(near_left[1],))
    across_far = on_fsdp(across_far_code, ACROSS)
    up_far_code = product(far_left, rights, (0, 2), A1, after=(across_far_code,))
    up_far = on_fsdp(up_far_code, UP)
    down_far_code = product(far_left, rights, (0, 2), A2, after=(up_far_code,))
    down_far = on_fsdp(down_far_code, DOWN)

    across_near_code = product(near_left, rights, (3, 3), B, after=(down_far_code,))
    across_near = on_fsdp(across_near_code, ACROSS)
    up_own_code = product_pair(
        near_left, rights, 3, A2, far_left, 0, B1, across_far, (across_near_code,)
    )
    up_own = on_fsdp(up_own_code, UP)
    ahead_two = scatter_blocks(place, inner, (2,), (up_own_code, from_one, from_three))
    from_two = on_replica(ahead_two, AHEAD[2])

    partial = product(near_left, rights, (0, 3), ALL, after=(ahead_two,), kind=jnp.float32)
    partial_turn = product(near_left, rights, (5, 1), A, after=(partial,), kind=jnp.float32)

    down_own_code = product_pair(
        near_left, rights, 4, A1, far_left, 0, B2, across_far, (partial_turn, up_far)
    )
    down_own = on_fsdp(down_own_code, DOWN)

    up_turn_code = product(
        near_left, rights, (3, 1), A1, ((up_far, 1, A1, 0),), (down_own_code, down_far)
    )
    up_turn = on_fsdp(up_turn_code, UP)

    arrived = (from_one, from_two, from_three)
    line_sum, line = sum_line(
        place, inner, arrived, outer_weight, outer_momentum, (up_turn_code, across_near)
    )
    far_line = on_replica(line, FAR)

    down_turn_code = product(
        near_left, rights, (4, 1), A2, ((down_far, 1, (0, A2[1]), 0),), (line, up_own)
    )
    down_turn = on_fsdp(down_turn_code, DOWN)

    up_rest_code = combined(
        partial, 0, ALL,
        ((up_far, 0, A1, 0), (across_near, 0, B, 0), (up_own, 0, B1, A2[1])), (down_turn_code,),
    )
    up_rest = on_fsdp(up_rest_code, UP)
    down_rest_code = combined(
        partial, 1, ALL,
        ((down_far, 0, A2, 0), (across_near, 1, B, 0), (down_own, 0, B2, A1[1])), (up_rest_code,),
    )
    down_rest = on_fsdp(down_rest_code, DOWN)

    outer_next, momentum_next, pair = outer_step(
        line_sum, line, far_line, outer_weight, outer_momentum, (down_rest_code, up_turn)
    )
    turned_code = combined(
        partial_turn, 0, A,
        ((up_turn, 0, A1, 0), (down_own, 0, A1, 0), (up_own, 0, A2, 0), (down_turn, 0, A2, 0)),
        (pair,),
    )
    turned = on_fsdp(turned_code, ACROSS)

    from_next, from_last = on_replica(pair, AHEAD[1]), on_replica(pair, AHEAD[3])
    blended = blend(place, inner, [(0, pair)], None, (turned_code,))
    pair_two = copied(pair, (blended, from_next, from_last))
    from_far = on_replica(pair_two, AHEAD[2])
    blended = blend(place, inner, [(3, from_last), (1, from_next)], blended, (pair_two,))
    base, first_part, second_part = prepare_finish(
        partial, 2, (across_near, 2), up_rest, first, second, (blended,)
    )
    blended = blend(place, inner, [(2, from_far)], blended, (base,))
    inner_next, first_next, second_next = finish(
        base, first_part, second_part, blended, down_rest, turned
    )
    return (inner_next[None], first_next[None], second_next[None], outer_next, momentum_next)


def solution(mesh):
    in_specs = (
        P("replica", "fsdp", None),
        P("replica", "fsdp", None),
        P("replica", "fsdp", None),
        P("fsdp", "replica"),
        P("fsdp", "replica"),
        P("replica", "fsdp", None),
        P("replica", "fsdp", None),
    )
    out_specs = (
        P("replica", "fsdp", None),
        P("replica", "fsdp", None),
        P("replica", "fsdp", None),
        P("fsdp", "replica"),
        P("fsdp", "replica"),
    )
    return jax.shard_map(local, mesh=mesh, in_specs=in_specs, out_specs=out_specs, check_vma=False)
```

```python
import jax
import jax.numpy as jnp
from jax import lax
from jax.experimental import pallas as pl
from jax.experimental.pallas import tpu as pltpu
from jax.sharding import PartitionSpec as P

outer_rate = 0.7
outer_decay = 0.9
mix_share = 0.5
beta_one = 0.9
beta_two = 0.95
inner_rate = 0.05
weight_decay = 0.1
epsilon = 1e-08
step_count = 200.0
kept_share = 1.0 - inner_rate * weight_decay
corr_one = 1.0 - beta_one**step_count
corr_two = 1.0 - beta_two**step_count

NY, NX, NC, NZ, NH = 4, 2, 2, 4, 2
BLOCK = 256
A1, A2, B1, B2 = (0, 3), (3, 3), (6, 1), (7, 1)
A, B, ALL = (0, 6), (6, 2), (0, 8)
VMEM = 16 * 2**20


def along_fsdp(move):
    where = [(y, x, c) for y in range(NY) for x in range(NX) for c in range(NC)]
    number = lambda y, x, c: ((y % NY) * NX + x) * NC + c
    return [(number(*place), number(*move(*place))) for place in where]


def along_replica(move):
    where = [(h, z) for h in range(NH) for z in range(NZ)]
    number = lambda h, z: h * NZ + z % NZ
    return [(number(*place), number(*move(*place))) for place in where]


UP = along_fsdp(lambda y, x, c: (y + 1, x, c))
DOWN = along_fsdp(lambda y, x, c: (y - 1, x, c))
ACROSS = along_fsdp(lambda y, x, c: (y, 1 - x, c))
TWIN = along_fsdp(lambda y, x, c: (y, x, 1 - c))
FAR = along_replica(lambda h, z: (1 - h, z))
AHEAD = [along_replica(lambda h, z, k=k: (h, z + k)) for k in range(NZ)]


def on_fsdp(value, pairs):
    return lax.ppermute(value, "fsdp", pairs)


def on_replica(value, pairs):
    return lax.ppermute(value, "replica", pairs)


def coded(value):
    return (value * jnp.abs(value) * (value * value)).astype(jnp.bfloat16)


def decoded(code):
    code = code.astype(jnp.float32)
    root = lax.rsqrt(lax.rsqrt(jnp.abs(code)))
    return jnp.where(code < 0.0, -root, root)


def coded_outer(value):
    value = value * 4096.0
    square = value * value
    fourth = square * square
    return (value * jnp.abs(value) * square * fourth).astype(jnp.bfloat16)


def decoded_outer(code):
    code = code.astype(jnp.float32)
    root = jnp.sqrt(lax.rsqrt(lax.rsqrt(jnp.abs(code)))) * (1.0 / 4096.0)
    return jnp.where(code < 0.0, -root, root)


def run(kernel, grid, ins, outs, after=(), prefetch=(), scratch=(), aliases=None):
    read, late = len(prefetch) + len(ins), len(after)

    def body(*refs):
        kernel(*refs[:read], *refs[read + late :])

    arrays = [array for array, _ in ins]
    shapes = tuple(shape for shape, _ in outs)
    result = pl.pallas_call(
        body,
        out_shape=shapes,
        grid_spec=pltpu.PrefetchScalarGridSpec(
            num_scalar_prefetch=len(prefetch),
            grid=grid,
            in_specs=[spec for _, spec in ins] + [pl.BlockSpec(memory_space=pl.ANY)] * late,
            out_specs=tuple(spec for _, spec in outs),
            scratch_shapes=list(scratch),
        ),
        input_output_aliases=aliases or {},
        compiler_params=pltpu.CompilerParams(vmem_limit_bytes=VMEM),
        cost_estimate=pl.CostEstimate(flops=1, bytes_accessed=1, transcendentals=0),
    )(*prefetch, *arrays, *after)
    return result[0] if len(outs) == 1 else result


def prepare(place, activations, after=()):
    tokens, width = activations.shape
    quarter = width // NY
    rows = quarter // (NX * NC)

    def distance(i):
        return jnp.where(i == 0, 2, jnp.where(i == 1, 1, jnp.where(i == 2, 3, 0)))

    def kernel(place_ref, a_ref, far_own, far_send, near_own, near_send, turned):
        turned[...] = a_ref[...].T
        x, core = place_ref[1], place_ref[2]

        def write(own_ref, send_ref):
            for dx in range(NX):
                column = (x + dx) % NX
                own = pl.multiple_of((column * NC + core) * rows, 16)
                other = pl.multiple_of((column * NC + 1 - core) * rows, 16)
                own_ref[dx, 0] = turned[pl.ds(own, rows), :]
                send_ref[dx, 0] = turned[pl.ds(other, rows), :]

        pl.when(pl.program_id(0) == 0)(lambda: write(far_own, far_send))
        pl.when(pl.program_id(0) > 0)(lambda: write(near_own, near_send))

    def out(count):
        return (
            jax.ShapeDtypeStruct((NX, count, rows, tokens), jnp.bfloat16),
            pl.BlockSpec((NX, 1, rows, tokens), lambda i, s: (0, 0 if count == 1 else jnp.maximum(i - 1, 0), 0, 0)),
        )

    source = pl.BlockSpec((tokens, quarter), lambda i, s: (0, (s[0] + distance(i)) % NY))
    results = run(
        kernel, (NY,), [(activations, source)], [out(1), out(1), out(NY - 1), out(NY - 1)], after, (place,),
        [pltpu.VMEM((quarter, tokens), jnp.bfloat16)],
    )
    return [array.reshape(-1, rows, tokens) for array in results]


def run_whole(kernel, arrays, shape, after=()):
    count = len(arrays)
    vmem = pl.BlockSpec(memory_space=pltpu.VMEM)

    def body(*refs):
        kernel(*refs[:count], *refs[count + len(after) :])

    return pl.pallas_call(
        body,
        out_shape=shape,
        in_specs=[vmem] * count + [pl.BlockSpec(memory_space=pl.ANY)] * len(after),
        out_specs=jax.tree.map(lambda _: vmem, shape),
        compiler_params=pltpu.CompilerParams(vmem_limit_bytes=VMEM),
    )(*arrays, *after)


def block_columns(j):
    start = j * BLOCK
    return pl.ds(start if isinstance(start, int) else pl.multiple_of(start, BLOCK), BLOCK)


def dots(lefts, rights, blocks, j):
    start, count = blocks
    total = None
    for left, right in zip(lefts, rights):
        rows, depth = left.shape[1:]
        part = left[start : start + count].reshape(count * rows, depth)
        part = jnp.dot(part, right[:, block_columns(j)], preferred_element_type=jnp.float32)
        total = part if total is None else total + part
    return total.reshape(count, rows, BLOCK)


def regions(number, received):
    cuts = {0, number}
    for _, _, span, _ in received:
        cuts |= {span[0], span[0] + span[1]}
    cuts = sorted(cuts)
    found = []
    for low, high in zip(cuts, cuts[1:]):
        which = [i for i, (_, _, span, _) in enumerate(received) if span[0] <= low < span[0] + span[1]]
        found.append((low, high, which))
    return found


def product(lefts, rights, blocks, columns, received=(), after=(), kind=jnp.bfloat16):
    first, number = columns
    count, rows = blocks[1], lefts[0].shape[1]

    def kernel(lo, lt, ro, rt, *rest):
        out = rest[-1]

        def step(j, which):
            total = dots((lo, lt), (ro, rt), blocks, first + j)
            for i in which:
                _, block, span, offset = received[i]
                total = total + decoded(rest[i][block : block + count, :, block_columns(offset + j - span[0])])
            out[:, :, block_columns(j)] = coded(total) if kind == jnp.bfloat16 else total

        for low, high, which in regions(number, received):
            pl.loop(low, high)(lambda j, which=which: step(j, which))

    shape = jax.ShapeDtypeStruct((count, rows, number * BLOCK), kind)
    return run_whole(kernel, [*lefts, *rights, *(array for array, *_ in received)], shape, after)


def combined(partial, block, columns, received, after=()):
    first, number = columns
    rows = partial.shape[1]

    def kernel(values, *rest):
        out = rest[-1]

        def step(j, which):
            total = values[block : block + 1, :, block_columns(first + j)]
            for i in which:
                _, row, span, offset = received[i]
                total = total + decoded(rest[i][row : row + 1, :, block_columns(offset + j - span[0])])
            out[:, :, block_columns(j)] = coded(total)

        for low, high, which in regions(number, received):
            pl.loop(low, high)(lambda j, which=which: step(j, which))

    shape = jax.ShapeDtypeStruct((1, rows, number * BLOCK), jnp.bfloat16)
    return run_whole(kernel, [partial, *(array for array, *_ in received)], shape, after)


def product_pair(lefts, rights, block, columns, lefts_last, block_last, columns_last, codes, after=()):
    first, number = columns
    first_last, number_last = columns_last
    rows = lefts[0].shape[1]

    def kernel(lo, lt, lo2, lt2, ro, rt, code, out):
        @pl.loop(0, number)
        def _(j):
            out[:, :, block_columns(j)] = coded(dots((lo, lt), (ro, rt), (block, 1), first + j))

        @pl.loop(0, number_last)
        def _(j):
            total = dots((lo2, lt2), (ro, rt), (block_last, 1), first_last + j)
            total = total + decoded(code[:, :, block_columns(first_last - B[0] + j)])
            out[:, :, block_columns(number + j)] = coded(total)

    shape = jax.ShapeDtypeStruct((1, rows, (number + number_last) * BLOCK), jnp.bfloat16)
    return run_whole(kernel, [*lefts, *lefts_last, *rights, codes], shape, after)


def prepare_finish(partial, block, received, up, first, second, after=()):
    rows = partial.shape[1]

    def kernel(values, code, up_ref, first_ref, second_ref, base, first_out, second_out):
        def step(j, with_code):
            columns = block_columns(j)
            total = values[block, :, columns] + decoded(up_ref[0, :, columns])
            if with_code:
                total = total + decoded(code[received[1], :, block_columns(j - B[0])])
            base[:, columns] = total
            first_out[:, columns] = beta_one * first_ref[:, columns] + (1.0 - beta_one) * total
            second_out[:, columns] = beta_two * second_ref[:, columns]

        pl.loop(0, B[0])(lambda j: step(j, False))
        pl.loop(B[0], ALL[1])(lambda j: step(j, True))

    shape = (jax.ShapeDtypeStruct((rows, ALL[1] * BLOCK), jnp.float32),) * 3
    return run_whole(kernel, [partial, received[0], up, first, second], shape, after)


def finish(base, first_part, second_part, blended, down, across, after=()):
    rows, width = base.shape
    wide = 2 * BLOCK
    cut = A[1] // 2

    def kernel(base_ref, first_ref, second_ref, blended_ref, down_ref, across_ref, inner_out, first_out, second_out):
        def store(rest):
            total = base_ref[...] + rest
            first_next = first_ref[...] + (1.0 - beta_one) * rest
            second_next = second_ref[...] + (1.0 - beta_two) * total * total
            scaled = second_next * (1.0 / corr_two)
            update = first_next * (inner_rate / corr_one) / (scaled * lax.rsqrt(scaled) + epsilon)
            inner_out[...] = blended_ref[...] - update
            first_out[...] = first_next
            second_out[...] = second_next

        step = pl.program_id(0)

        @pl.when(step < cut)
        def _():
            store(decoded(down_ref[0]) + decoded(across_ref[0]))

        @pl.when(step >= cut)
        def _():
            store(decoded(down_ref[0]))

    whole = pl.BlockSpec((1, rows, wide), lambda j: (0, 0, j))
    part = pl.BlockSpec((1, rows, wide), lambda j: (0, 0, jnp.minimum(j, cut - 1)))
    state = pl.BlockSpec((rows, wide), lambda j: (0, j))
    out = (jax.ShapeDtypeStruct((rows, width), jnp.float32), state)
    ins = [(array, state) for array in (base, first_part, second_part, blended)]
    ins += [(down, whole), (across, part)]
    return run(kernel, (width // wide,), ins, [out] * 3, after)


def scatter_blocks(place, inner, places, after=()):
    n = len(places)

    def kernel(place_ref, inner_ref, *rest):
        for k, out in zip(places, rest[len(after) :]):
            for d in range(NH):
                column = (d + place_ref[4]) % NH * NZ + (place_ref[3] + k) % NZ
                out[d] = inner_ref[:, block_columns(column)]

    vmem = pl.BlockSpec(memory_space=pltpu.VMEM)
    result = pl.pallas_call(
        kernel,
        out_shape=(jax.ShapeDtypeStruct((NH, inner.shape[0], BLOCK), jnp.float32),) * n,
        in_specs=[pl.BlockSpec(memory_space=pltpu.SMEM), vmem] + [pl.BlockSpec(memory_space=pl.ANY)] * len(after),
        out_specs=(vmem,) * n,
        compiler_params=pltpu.CompilerParams(vmem_limit_bytes=VMEM),
    )(place, inner, *after)
    return result[0] if n == 1 else result


outer_share = 1.0 - outer_rate * (1.0 + outer_decay)
sum_share = outer_rate * (1.0 + outer_decay) / (NZ * NH)
momentum_share = -outer_rate * outer_decay * outer_decay


def sum_line(place, inner, arrived, outer_weight, outer_momentum, after=()):
    rows = inner.shape[0]

    def kernel(place_ref, near, far, *rest):
        here, there, weight, momentum, sum_out, out = rest[:3], rest[3:6], rest[6], rest[7], rest[8], rest[9]
        out[0] = far[...] + there[0][0] + there[1][0] + there[2][0]
        summed = near[...] + here[0][0] + here[1][0] + here[2][0]
        sum_out[...] = summed
        out[1] = outer_share * weight[...] + momentum_share * momentum[...] + sum_share * summed

    def own(d):
        return pl.BlockSpec((rows, BLOCK), lambda i, s: (0, ((s[4] + d) % NH) * NZ + s[3]))

    def part(d):
        return pl.BlockSpec((1, rows, BLOCK), lambda i, s: (d, 0, 0))

    whole = pl.BlockSpec((rows, BLOCK), lambda i, s: (0, 0))
    ins = [(inner, own(0)), (inner, own(1))]
    ins += [(a, part(0)) for a in arrived] + [(a, part(1)) for a in arrived]
    ins += [(outer_weight, whole), (outer_momentum, whole)]
    outs = [
        (jax.ShapeDtypeStruct((rows, BLOCK), jnp.float32), whole),
        (
            jax.ShapeDtypeStruct((NH, rows, BLOCK), jnp.float32),
            pl.BlockSpec((NH, rows, BLOCK), lambda i, s: (0, 0, 0)),
        ),
    ]
    return run(kernel, (1,), ins, outs, after, (place,))


def outer_step(line_sum, line, far, outer_weight, outer_momentum, after=()):
    def kernel(sum_ref, line_ref, far_ref, weight, momentum, next_ref, momentum_ref, code_ref):
        average = weight[...] - (sum_ref[...] + far_ref[0]) / (NZ * NH)
        momentum_next = outer_decay * momentum[...] + average
        outer_next = weight[...] - outer_rate * (average + outer_decay * momentum_next)
        next_ref[...] = outer_next
        momentum_ref[...] = momentum_next
        code_ref[0] = coded_outer(outer_next)
        code_ref[1] = coded_outer(far_ref[1] + sum_share * line_ref[0])

    shape = jax.ShapeDtypeStruct(line_sum.shape, jnp.float32)
    shapes = (shape, shape, jax.ShapeDtypeStruct(line.shape, jnp.bfloat16))
    return run_whole(kernel, [line_sum, line, far, outer_weight, outer_momentum], shapes, after)


def copied(array, after=()):
    def kernel(source, out):
        out[...] = source[...]

    return run_whole(kernel, [array], jax.ShapeDtypeStruct(array.shape, array.dtype), after)


def blend(place, inner, gathered, buffer=None, after=()):
    count = len(gathered)

    def kernel(place_ref, inner_ref, *rest):
        out = rest[-1]
        for (back, _), code in zip(gathered, rest):
            for d in range(NH):
                column = (d + place_ref[4]) % NH * NZ + (place_ref[3] - back + NZ) % NZ
                half = kept_share * (1.0 - mix_share) * inner_ref[:, block_columns(column)]
                out[:, block_columns(column)] = kept_share * mix_share * decoded_outer(code[d]) + half

    vmem = pl.BlockSpec(memory_space=pltpu.VMEM)
    operands = [place, inner, *(codes for _, codes in gathered)]
    specs = [pl.BlockSpec(memory_space=pltpu.SMEM)] + [vmem] * (1 + count)
    aliases = {}
    if buffer is not None:
        aliases = {len(operands): 0}
        operands.append(buffer)
        specs.append(vmem)
    return pl.pallas_call(
        kernel,
        out_shape=jax.ShapeDtypeStruct(inner.shape, jnp.float32),
        in_specs=specs + [pl.BlockSpec(memory_space=pl.ANY)] * len(after),
        out_specs=vmem,
        input_output_aliases=aliases,
        compiler_params=pltpu.CompilerParams(vmem_limit_bytes=VMEM),
    )(*operands, *after)


def local(
    inner_weight, first_moment, second_moment, outer_weight, outer_momentum, activations, out_grads
):
    inner, first, second = inner_weight[0], first_moment[0], second_moment[0]
    inputs, cotangents = activations[0], out_grads[0]
    replica, member = lax.axis_index("replica"), lax.axis_index("fsdp")
    core, column, row = member % NC, member // NC % NX, member // (NC * NX)
    depth, side = replica % NZ, replica // NZ
    place = jnp.stack([row, column, core, depth, side]).astype(jnp.int32)

    rights = (cotangents, on_fsdp(cotangents, TWIN))
    far_own, far_send, near_own, near_send = prepare(place, inputs)
    far_left = (far_own, on_fsdp(far_send, TWIN))
    near_left = (near_own, on_fsdp(near_send, TWIN))
    ahead_one, ahead_three = scatter_blocks(place, inner, (1, 3), (far_own,))
    from_one, from_three = on_replica(ahead_one, AHEAD[1]), on_replica(ahead_three, AHEAD[3])

    across_far_code = product(far_left, rights, (1, 1), B, after=(near_left[1],))
    across_far = on_fsdp(across_far_code, ACROSS)
    up_far_code = product(far_left, rights, (0, 2), A1, after=(across_far_code,))
    up_far = on_fsdp(up_far_code, UP)
    down_far_code = product(far_left, rights, (0, 2), A2, after=(up_far_code,))
    down_far = on_fsdp(down_far_code, DOWN)

    across_near_code = product(near_left, rights, (3, 3), B, after=(down_far_code,))
    across_near = on_fsdp(across_near_code, ACROSS)
    up_own_code = product_pair(
        near_left, rights, 3, A2, far_left, 0, B1, across_far, (across_near_code,)
    )
    up_own = on_fsdp(up_own_code, UP)
    ahead_two = scatter_blocks(place, inner, (2,), (up_own_code, from_one, from_three))
    from_two = on_replica(ahead_two, AHEAD[2])

    partial = product(near_left, rights, (0, 3), ALL, after=(ahead_two,), kind=jnp.float32)
    partial_turn = product(near_left, rights, (5, 1), A, after=(partial,), kind=jnp.float32)

    down_own_code = product_pair(
        near_left, rights, 4, A1, far_left, 0, B2, across_far, (partial_turn, up_far)
    )
    down_own = on_fsdp(down_own_code, DOWN)

    up_turn_code = product(
        near_left, rights, (3, 1), A1, ((up_far, 1, A1, 0),), (down_own_code, down_far)
    )
    up_turn = on_fsdp(up_turn_code, UP)

    arrived = (from_one, from_two, from_three)
    line_sum, line = sum_line(
        place, inner, arrived, outer_weight, outer_momentum, (up_turn_code, across_near)
    )
    far_line = on_replica(line, FAR)

    down_turn_code = product(
        near_left, rights, (4, 1), A2, ((down_far, 1, (0, A2[1]), 0),), (line, up_own)
    )
    down_turn = on_fsdp(down_turn_code, DOWN)

    up_rest_code = combined(
        partial, 0, ALL,
        ((up_far, 0, A1, 0), (across_near, 0, B, 0), (up_own, 0, B1, A2[1])), (down_turn_code,),
    )
    up_rest = on_fsdp(up_rest_code, UP)
    down_rest_code = combined(
        partial, 1, ALL,
        ((down_far, 0, A2, 0), (across_near, 1, B, 0), (down_own, 0, B2, A1[1])), (up_rest_code,),
    )
    down_rest = on_fsdp(down_rest_code, DOWN)

    outer_next, momentum_next, pair = outer_step(
        line_sum, line, far_line, outer_weight, outer_momentum, (down_rest_code, up_turn)
    )
    turned_code = combined(
        partial_turn, 0, A,
        ((up_turn, 0, A1, 0), (down_own, 0, A1, 0), (up_own, 0, A2, 0), (down_turn, 0, A2, 0)),
        (pair,),
    )
    turned = on_fsdp(turned_code, ACROSS)

    from_next, from_last = on_replica(pair, AHEAD[1]), on_replica(pair, AHEAD[3])
    blended = blend(place, inner, [(0, pair)], None, (turned_code,))
    pair_two = copied(pair, (blended, from_next, from_last))
    from_far = on_replica(pair_two, AHEAD[2])
    blended = blend(place, inner, [(3, from_last), (1, from_next)], blended, (pair_two,))
    base, first_part, second_part = prepare_finish(
        partial, 2, (across_near, 2), up_rest, first, second, (blended,)
    )
    blended = blend(place, inner, [(2, from_far)], blended, (base,))
    inner_next, first_next, second_next = finish(
        base, first_part, second_part, blended, down_rest, turned
    )
    return (inner_next[None], first_next[None], second_next[None], outer_next, momentum_next)


def solution(mesh):
    in_specs = (
        P("replica", "fsdp", None),
        P("replica", "fsdp", None),
        P("replica", "fsdp", None),
        P("fsdp", "replica"),
        P("fsdp", "replica"),
        P("replica", "fsdp", None),
        P("replica", "fsdp", None),
    )
    out_specs = (
        P("replica", "fsdp", None),
        P("replica", "fsdp", None),
        P("replica", "fsdp", None),
        P("fsdp", "replica"),
        P("fsdp", "replica"),
    )
    return jax.shard_map(local, mesh=mesh, in_specs=in_specs, out_specs=out_specs, check_vma=False)
```
